32 devices in a mesh: bus: 8 (over z, x), case: 4 (over y, core).
Axes of the slice: x: 2, y: 2, z: 4, core: 2. Of those that a mesh axis runs over, the one named last changes fastest.
Arguments:
- z_columns: float32 [8192, 1024], P('bus')
- resident_bus: int32 [1024], replicated, may hold values from 0 to 8191, as said below
- fault_col: int32 [2048], P('case'), may hold values from 0 to 1023
- switch_cols: int32 [2048, 2], P('case'), may hold values from 0 to 1023, as said below
- tie_x: float32 [2048], P('case'), may hold values from 0.5 to 2
- fault_z: float32 [2048], P('case'), may hold values from 0.5 to 2
- boundary_send: int32 [8, 2, 128], replicated, may hold values from 0 to 1023, as said below
- branch_ends: int32 [12288, 2], P('bus'), may hold values from 0 to 1279, as said below
- branch_x: float32 [12288], P('bus'), may hold values from 0.01 to 0.05
- pickup: float32 [12288], P('bus'), may hold values from 0.2 to 1.5
- tds: float32 [12288], P('bus'), may hold values from 0.05 to 0.5
- curve: int32 [12288], P('bus'), may hold values from 0 to 2
Outputs:
- voltage: float32 [8192, 2048], P('bus', 'case')
- relay_rate: float32 [12288, 2048], P('bus', 'case')
- worst_rate: float32 [12288], P('bus')
The draws below stay inside these ranges and needn't reach their ends.
Inputs may be any that keep to these rules, and one draw needn't show every extreme that they name: `resident_bus`: distinct bus ids. `switch_cols`: the two columns of a case differ. `boundary_send`: rows sent to the lower block lie among the first 256 rows, rows sent to the upper block among the last 256; each block's live slots come first and hold distinct rows, padding repeats the first slot's row; the first block sends nothing down and the last nothing up; some block fills all 128 slots. `branch_ends`: a to slot of 1024 or more points at a live slot of the neighbour's block; the first block never uses the lower slots, the last never the upper ones; a local to row differs from the from row.
All inputs are finite; a program needn't handle non-finite values.
Results may differ from the reference program's by a relative error of at most 0.000049.
Values sent between devices are 32-bit elements; how exact they have to be, the bound alone decides.
No kernel may reach another device: no remote copies, remote signals or barrier semaphores. Data moves between devices by JAX's collectives and lax.ppermute only.
A program may use at most 64 MiB of HBM per device.

```python
import math
import jax
import jax.numpy as jnp
from jax import lax

BUS_DEV = 1024
K = 1024
CASE_DEV = 512
BR_DEV = 1536
HB = 128
RIM = 256
NB = 8192
NBR = 12288
CASES = 2048
N_BUS = 8


def resident_ids(key):
    return jax.random.permutation(jax.random.fold_in(key, 11), NB)[:K].astype(jnp.int32)


def draw_resident_bus(key, part):
    return resident_ids(key)


def draw_z_columns(key, part):
    resident = resident_ids(key)
    noise_key = jax.random.fold_in(key, 12)
    noise = jnp.clip(0.04 * jax.random.normal(noise_key, (NB, K), jnp.float32), -0.24, 0.24)
    diagonal = jax.random.uniform(jax.random.fold_in(key, 13), (K,), jnp.float32, 2.0, 4.0)
    return noise.at[resident, jnp.arange(K)].add(diagonal)


def draw_switch_cols(key, part):
    first_col = jax.random.randint(jax.random.fold_in(key, 21), (CASES,), 0, K)
    offset_col = jax.random.randint(jax.random.fold_in(key, 22), (CASES,), 1, K)
    return jnp.stack([first_col, (first_col + offset_col) % K], axis=1).astype(jnp.int32)


def topology(key):
    shards = NB // BUS_DEV
    counts = jax.random.randint(jax.random.fold_in(key, 31), (shards, 2), HB // 2, HB + 1)
    counts = counts.at[1, 0].set(HB).at[0, 1].set(HB).at[0, 0].set(0).at[shards - 1, 1].set(0)
    scores = jax.random.randint(jax.random.fold_in(key, 32), (shards, 2, RIM), 0, 1048576) * RIM + jnp.arange(RIM, dtype=jnp.int32)
    chosen = jnp.argsort(scores, axis=-1)[..., :HB].astype(jnp.int32)
    chosen = chosen + jnp.array([0, BUS_DEV - RIM], jnp.int32)[None, :, None]
    slot_ids = jnp.arange(HB, dtype=jnp.int32)[None, None, :]
    send_rows = jnp.where(slot_ids < counts[:, :, None], chosen, chosen[..., :1])
    branch = jnp.arange(NBR, dtype=jnp.int32)
    owner = branch // BR_DEV
    position = branch % BR_DEV
    anchor = jax.random.randint(jax.random.fold_in(key, 33), (NBR,), 0, BUS_DEV)
    local_to = (anchor + jax.random.randint(jax.random.fold_in(key, 34), (NBR,), 1, BUS_DEV)) % BUS_DEV
    draw_r = jax.random.randint(jax.random.fold_in(key, 35), (NBR,), 0, 1048576)
    go_lower = (position % 2 == 0) & (owner > 0) | (owner == shards - 1)
    lower_count = counts[jnp.maximum(owner - 1, 0), 1]
    upper_count = counts[jnp.minimum(owner + 1, shards - 1), 0]
    lower_slot = BUS_DEV + draw_r % jnp.maximum(lower_count, 1)
    upper_slot = BUS_DEV + HB + draw_r % jnp.maximum(upper_count, 1)
    target = jnp.where(position < BR_DEV // 4, jnp.where(go_lower, lower_slot, upper_slot), local_to)
    return (send_rows.astype(jnp.int32), jnp.stack([anchor, target], axis=1).astype(jnp.int32))


def draw_boundary_send(key, part):
    return topology(key)[0]


def draw_branch_ends(key, part):
    return topology(key)[1]


def place_ends(result, stream_key, least, top_value):
    spot = [jax.random.randint(jax.random.fold_in(stream_key, axis), (), 0, length) for axis, length in enumerate(result.shape)]
    widest = result.shape.index(max(result.shape))
    beside = spot[:widest] + [(spot[widest] + 1) % result.shape[widest]] + spot[widest + 1:]
    return result.at[tuple(spot)].set(least).at[tuple(beside)].set(top_value)


def block_scale(stream_key, shape, split, smallest, largest):
    gain = 1.0
    for dim, parts in split:
        steps = jax.random.uniform(jax.random.fold_in(jax.random.fold_in(stream_key, 6), dim), (parts,), jnp.float32, smallest / len(split), largest / len(split))
        gain = gain * jnp.repeat(jnp.exp(steps), shape[dim] // parts).reshape((-1,) + (1,) * (len(shape) - 1 - dim))
    return gain


def setup_inputs(seed: int = 0) -> dict:
    keys = jax.random.split(jax.random.key(seed), 13)
    return {
        "z_columns": draw_z_columns(jax.random.fold_in(keys[12], 71), 0),
        "resident_bus": draw_resident_bus(jax.random.fold_in(keys[12], 71), 0),
        "fault_col": place_ends(jax.random.randint(keys[2], (CASES,), 0, K), jax.random.fold_in(keys[2], 1), 0, K - 1).astype(jnp.int32),
        "switch_cols": draw_switch_cols(jax.random.fold_in(keys[12], 71), 0),
        "tie_x": jnp.clip(jnp.exp(math.log(2.0) - 1.3862944 * jax.random.uniform(keys[4], (CASES,), jnp.float32) ** block_scale(keys[4], (CASES,), ((0, 4),), -0.2, 0.2)), 0.5, 2.0),
        "fault_z": jnp.clip(jnp.exp(math.log(2.0) - 1.3862944 * jax.random.uniform(keys[5], (CASES,), jnp.float32) ** block_scale(keys[5], (CASES,), ((0, 4),), -0.2, 0.2)), 0.5, 2.0),
        "boundary_send": draw_boundary_send(jax.random.fold_in(keys[12], 71), 0),
        "branch_ends": draw_branch_ends(jax.random.fold_in(keys[12], 71), 0),
        "branch_x": jnp.clip(jnp.exp(math.log(0.05) - 1.609438 * jax.random.uniform(keys[8], (NBR,), jnp.float32) ** block_scale(keys[8], (NBR,), ((0, 8),), -0.2, 0.2)), 0.01, 0.05),
        "pickup": jnp.clip(jnp.exp(math.log(1.5) - 2.014903 * jax.random.uniform(keys[9], (NBR,), jnp.float32) ** block_scale(keys[9], (NBR,), ((0, 8),), -0.2, 0.2)), 0.2, 1.5),
        "tds": jnp.clip(jnp.exp(math.log(0.5) - 2.3025851 * jax.random.uniform(keys[10], (NBR,), jnp.float32) ** block_scale(keys[10], (NBR,), ((0, 8),), -0.2, 0.2)), 0.05, 0.5),
        "curve": place_ends(jax.random.randint(keys[11], (NBR,), 0, 3), jax.random.fold_in(keys[11], 1), 0, 2).astype(jnp.int32),
    }


def relay_of(currents, pickup, tds, curve):
    factor = jnp.where(curve == 0, 0.14, jnp.where(curve == 1, 13.5, 80.0)).astype(jnp.float32)
    exponent = jnp.where(curve == 0, 0.02, jnp.where(curve == 1, 1.0, 2.0)).astype(jnp.float32)
    scaled = currents / pickup[:, None]
    powered = jnp.exp(0.5 * exponent[:, None] * jnp.log(scaled * scaled + 1e-4))
    return jnp.maximum(powered - 1.0, 0.0) / (factor * tds)[:, None]


def reference(z_columns, resident_bus, fault_col, switch_cols, tie_x, fault_z, boundary_send, branch_ends, branch_x, pickup, tds, curve):
    count_br = branch_ends.shape[0]
    owner = (jnp.arange(count_br) // BR_DEV).astype(jnp.int32)
    from_bus = owner * BUS_DEV + branch_ends[:, 0]
    to_slot = branch_ends[:, 1]
    lower_idx = jnp.clip(owner - 1, 0, N_BUS - 1)
    upper_idx = jnp.clip(owner + 1, 0, N_BUS - 1)
    low_slot = jnp.clip(to_slot - BUS_DEV, 0, HB - 1)
    high_slot = jnp.clip(to_slot - BUS_DEV - HB, 0, HB - 1)
    to_lower = lower_idx * BUS_DEV + boundary_send[lower_idx, 1, low_slot]
    to_upper = upper_idx * BUS_DEV + boundary_send[upper_idx, 0, high_slot]
    to_bus = jnp.where(to_slot < BUS_DEV, owner * BUS_DEV + to_slot, jnp.where(to_slot < BUS_DEV + HB, to_lower, to_upper))
    groups = fault_col.shape[0] // CASE_DEV
    case_ids = jnp.arange(CASE_DEV)

    def case_block(inputs):
        fault_one, switch_one, tie_one, imped_one = inputs
        fault_cols = jnp.take(z_columns, fault_one, axis=1)
        branch_diff = jnp.take(z_columns, switch_one[:, 0], axis=1) - jnp.take(z_columns, switch_one[:, 1], axis=1)
        bus_a = resident_bus[switch_one[:, 0]]
        bus_b = resident_bus[switch_one[:, 1]]
        bus_f = resident_bus[fault_one]
        g_one = branch_diff[bus_a, case_ids] - branch_diff[bus_b, case_ids]
        g_two = branch_diff[bus_f, case_ids]
        g_three = fault_cols[bus_f, case_ids]
        weight_ratio = g_two / (tie_one + g_one)
        self_z = g_three - g_two * weight_ratio
        fault_amps = 1.0 / (self_z + imped_one)
        voltage = 1.0 - (fault_cols - branch_diff * weight_ratio[None, :]) * fault_amps[None, :]
        currents = (jnp.take(voltage, from_bus, axis=0) - jnp.take(voltage, to_bus, axis=0)) / branch_x[:, None]
        return voltage, relay_of(currents, pickup, tds, curve)

    volts, relays = lax.map(case_block, (fault_col.reshape(groups, CASE_DEV), switch_cols.reshape(groups, CASE_DEV, 2), tie_x.reshape(groups, CASE_DEV), fault_z.reshape(groups, CASE_DEV)))
    voltage = jnp.transpose(volts, (1, 0, 2)).reshape(volts.shape[1], groups * CASE_DEV)
    relay_rate = jnp.transpose(relays, (1, 0, 2)).reshape(relays.shape[1], groups * CASE_DEV)
    return voltage, relay_rate, jnp.max(relay_rate, axis=1)
```

```python
import jax
import jax.numpy as jnp
from jax import lax
from jax.experimental import pallas as pl
from jax.experimental.pallas import tpu as pltpu
from jax.sharding import PartitionSpec as P

RIM = 256
TILE = 256
F32 = jnp.float32
BF16 = jnp.bfloat16


def split_hi_lo(value):
    hi = value.astype(BF16)
    return hi, (value - hi.astype(F32)).astype(BF16)


def two_pass(hi, lo, rhs):
    return jnp.dot(hi, rhs, preferred_element_type=F32) + jnp.dot(
        lo, rhs, preferred_element_type=F32
    )


def send_kernel(meta_ref, z_ref, out_ref):
    for i in range(out_ref.shape[0]):
        out_ref[pl.ds(i, 1), :] = z_ref[pl.ds(meta_ref[1 + i], 1), :]


def gather_send_rows(z_columns, meta, piece):
    cols = z_columns.shape[1]
    return pl.pallas_call(
        send_kernel,
        grid_spec=pltpu.PrefetchScalarGridSpec(
            num_scalar_prefetch=1,
            grid=(1,),
            in_specs=[pl.BlockSpec((RIM, cols), lambda i, meta: (meta[0], 0))],
            out_specs=pl.BlockSpec((piece, cols), lambda i, meta: (0, 0)),
        ),
        out_shape=jax.ShapeDtypeStruct((piece, cols), F32),
        name="gather_send_rows",
    )(meta, z_columns)


def columns_kernel(z_hbm, cases_ref, resident_ref, fd_ref, pick_ref, g_ref, zbuf, sems):
    rows, cols = zbuf.shape
    cases = cases_ref.shape[1]
    tiles = rows // TILE
    copies = [
        pltpu.make_async_copy(
            z_hbm.at[pl.ds(t * TILE, TILE)], zbuf.at[pl.ds(t * TILE, TILE)], sems.at[t]
        )
        for t in range(tiles)
    ]
    for copy in copies:
        copy.start()
    f, a, b = cases_ref[0:1, :], cases_ref[1:2, :], cases_ref[2:3, :]
    for t in range(cols // TILE):
        k = lax.broadcasted_iota(jnp.int32, (TILE, cases), 0) + t * TILE
        span = pl.ds(t * TILE, TILE)
        pick_ref[span, :cases] = jnp.where(k == f, 1.0, 0.0).astype(BF16)
        pick_ref[span, cases:] = jnp.where(
            k == a, 1.0, jnp.where(k == b, -1.0, 0.0)
        ).astype(BF16)
    g1 = jnp.zeros((1, cases), F32)
    g2 = jnp.zeros((1, cases), F32)
    g3 = jnp.zeros((1, cases), F32)
    for t in range(tiles):
        span = pl.ds(t * TILE, TILE)
        row = lax.broadcasted_iota(jnp.int32, (TILE, cols), 0) + t * TILE
        k = lax.broadcasted_iota(jnp.int32, (TILE, cols), 1)
        owner = jnp.max(jnp.where(row == resident_ref[...], k, -1), axis=1, keepdims=True)
        copies[t].wait()
        hi, lo = split_hi_lo(zbuf[span, :])
        fd = two_pass(hi, lo, pick_ref[...])
        fd_ref[span, :] = fd
        fault, diff = fd[:, :cases], fd[:, cases:]
        at_f = owner == f
        g3 += jnp.sum(jnp.where(at_f, fault, 0.0), axis=0, keepdims=True)
        g2 += jnp.sum(jnp.where(at_f, diff, 0.0), axis=0, keepdims=True)
        g1 += jnp.sum(
            jnp.where(owner == a, diff, jnp.where(owner == b, -diff, 0.0)), axis=0, keepdims=True
        )
    g_ref[...] = jnp.broadcast_to(jnp.concatenate([g1, g2, g3])[None], g_ref.shape)


def pick_columns(z_columns, cases, resident, copies):
    rows, cols = z_columns.shape
    count = cases.shape[1]
    vmem = pl.BlockSpec(memory_space=pltpu.VMEM)
    return pl.pallas_call(
        columns_kernel,
        in_specs=[pl.BlockSpec(memory_space=pl.ANY), vmem, vmem],
        out_specs=[vmem, vmem, vmem],
        out_shape=[
            pltpu.VMEM((rows, 2 * count), F32),
            pltpu.VMEM((cols, 2 * count), BF16),
            jax.ShapeDtypeStruct((copies, 3, count), F32),
        ],
        scratch_shapes=[
            pltpu.VMEM((rows, cols), F32),
            pltpu.SemaphoreType.DMA((rows // TILE,)),
        ],
        compiler_params=pltpu.CompilerParams(vmem_limit_bytes=24 * 2**20),
        name="pick_columns",
    )(z_columns, cases, resident)


def branch_kernel(
    offsets,
    where_ref,
    g_ref,
    case_ref,
    fd_ref,
    pick_ref,
    par_ref,
    *refs,
):
    pieces = refs[: len(offsets)]
    volt_hbm, relay_hbm, worst_ref, vbuf, rbuf, zb, uh, ul, vsem, rsem = refs[len(offsets) :]
    rows, cases = vbuf.shape
    branches = rbuf.shape[0]
    ext = uh.shape[0]
    g = jnp.sum(g_ref[...], axis=0)
    g1, g2, g3 = g[0:1], g[1:2], g[2:3]
    ratio = g2 / (case_ref[0:1, :] + g1)
    amps = 1.0 / (g3 - g2 * ratio + case_ref[1:2, :])
    copies = []
    for t in range(rows // TILE):
        span = pl.ds(t * TILE, TILE)
        sag = (fd_ref[span, :cases] - fd_ref[span, cases:] * ratio) * amps
        vbuf[span, :] = 1.0 - sag
        copies.append(pltpu.make_async_copy(vbuf.at[span], volt_hbm.at[span], vsem.at[t]))
        copies[-1].start()
        uh[span, :], ul[span, :] = split_hi_lo(sag)
    for i, piece in enumerate(pieces):
        size = piece.shape[0]
        zb[pl.ds(pl.multiple_of(where_ref[i], size), size), :] = piece[...]
    hi, lo = split_hi_lo(zb[...])
    fd = two_pass(hi, lo, pick_ref[...])
    sag = (fd[:, :cases] - fd[:, cases:] * ratio) * amps
    span = pl.ds(rows, ext - rows)
    uh[span, :], ul[span, :] = split_hi_lo(sag)
    for t in range(branches // TILE):
        span = pl.ds(t * TILE, TILE)
        par = par_ref[span, :]
        bus = lax.broadcasted_iota(jnp.int32, (TILE, ext), 1).astype(F32)
        ends = jnp.where(
            bus == par[:, 1:2], 1.0, jnp.where(bus == par[:, 0:1], -1.0, 0.0)
        ).astype(BF16)
        drop = jnp.dot(ends, uh[...], preferred_element_type=F32) + jnp.dot(
            ends, ul[...], preferred_element_type=F32
        )
        scaled = drop * par[:, 2:3]
        square = scaled * scaled
        powered = jnp.exp2(par[:, 3:4] * jnp.log2(square + 1e-4))
        rbuf[span, :] = jnp.maximum(powered - 1.0, 0.0) * par[:, 4:5]
        copies.append(pltpu.make_async_copy(rbuf.at[span], relay_hbm.at[span], rsem.at[t]))
        copies[-1].start()
        largest = square[:, :128]
        for c in range(128, cases, 128):
            largest = jnp.maximum(largest, square[:, c : c + 128])
        for h in range(TILE // 128):
            worst_ref[pl.ds(t * (TILE // 128) + h, 1), :] = jnp.max(
                largest[h * 128 : (h + 1) * 128, :].T, axis=0, keepdims=True
            )
    for copy in copies:
        copy.wait()


def screen_branches(where, g_all, case_par, fd, pick, par, pieces, rows):
    count = case_par.shape[1]
    branches = par.shape[0]
    ext = rows + sum(piece.shape[0] for piece in pieces)
    vmem = pl.BlockSpec(memory_space=pltpu.VMEM)
    hbm = pl.BlockSpec(memory_space=pl.ANY)

    def kernel(*refs):
        branch_kernel(pieces, *refs)

    return pl.pallas_call(
        kernel,
        in_specs=[pl.BlockSpec(memory_space=pltpu.SMEM)] + [vmem] * (5 + len(pieces)),
        out_specs=[hbm, hbm, vmem],
        out_shape=[
            jax.ShapeDtypeStruct((rows, count), F32),
            jax.ShapeDtypeStruct((branches, count), F32),
            jax.ShapeDtypeStruct((branches // 128, 128), F32),
        ],
        scratch_shapes=[
            pltpu.VMEM((rows, count), F32),
            pltpu.VMEM((branches, count), F32),
            pltpu.VMEM((ext - rows, fd.shape[1]), F32),
            pltpu.VMEM((ext, count), BF16),
            pltpu.VMEM((ext, count), BF16),
            pltpu.SemaphoreType.DMA((rows // TILE,)),
            pltpu.SemaphoreType.DMA((branches // TILE,)),
        ],
        compiler_params=pltpu.CompilerParams(vmem_limit_bytes=40 * 2**20),
        name="screen_branches",
    )(where, g_all, case_par, fd, pick, par, *pieces)


def per_device(
    z_columns,
    resident_bus,
    fault_col,
    switch_cols,
    tie_x,
    fault_z,
    boundary_send,
    branch_ends,
    branch_x,
    pickup,
    tds,
    curve,
):
    rows = z_columns.shape[0]
    n_bus, n_case = lax.axis_size("bus"), lax.axis_size("case")
    my_bus, my_case = lax.axis_index("bus"), lax.axis_index("case")
    slots = boundary_send.shape[2]

    half = n_case // 2
    piece = slots // half
    down = my_case // half
    wanted = lax.dynamic_slice(
        boundary_send, (my_bus, 1 - down, (my_case % half) * piece), (1, 1, piece)
    )[0, 0]
    rim = (1 - down) * (rows // RIM - 1)
    meta = jnp.concatenate([rim[None], wanted - rim * RIM]).astype(jnp.int32)
    send = gather_send_rows(z_columns, meta, piece)
    pairs = []
    for s in range(n_bus):
        for c in range(n_case):
            to = s + 1 if c < half else s - 1
            if 0 <= to < n_bus:
                pairs.append((s * n_case + c, to * n_case + c))
    pieces = [lax.ppermute(send, ("bus", "case"), pairs)]
    masks = [0]

    cases = jnp.concatenate([fault_col[None], switch_cols.T], axis=0)
    resident = (resident_bus - my_bus * rows)[None]
    fd, pick, g_part = pick_columns(z_columns, cases, resident, n_bus)

    bit = n_case // 2
    while bit:
        swap = [(i, i ^ bit) for i in range(n_case)]
        pieces = pieces + [lax.ppermute(x, "case", swap) for x in pieces]
        masks = masks + [m ^ bit for m in masks]
        bit //= 2
    g_all = lax.all_to_all(g_part, "bus", 0, 0)

    where = jnp.stack([(my_case ^ m) * piece for m in masks]).astype(jnp.int32)
    gain = 1.0 / (branch_x * pickup)
    factor = jnp.where(curve == 0, 0.14, jnp.where(curve == 1, 13.5, 80.0)).astype(F32)
    power = jnp.where(curve == 0, 0.01, jnp.where(curve == 1, 0.5, 1.0)).astype(F32)
    rate = 1.0 / (factor * tds)
    zero = jnp.zeros_like(gain)
    par = jnp.stack(
        [
            branch_ends[:, 0].astype(F32),
            branch_ends[:, 1].astype(F32),
            gain,
            power,
            rate,
            zero,
            zero,
            zero,
        ],
        axis=1,
    )
    case_par = jnp.stack([tie_x, fault_z])
    voltage, relay_rate, square = screen_branches(
        where, g_all, case_par, fd, pick, par, pieces, rows
    )
    bit = 1
    while bit < n_case:
        square = jnp.maximum(
            square, lax.ppermute(square, "case", [(i, i ^ bit) for i in range(n_case)])
        )
        bit *= 2
    powered = jnp.exp2(power * jnp.log2(square.reshape(-1) + 1e-4))
    worst_rate = jnp.maximum(powered - 1.0, 0.0) * rate
    return (voltage, relay_rate, worst_rate)


def solution(mesh):
    in_specs = (
        P("bus", None),
        P(),
        P("case"),
        P("case", None),
        P("case"),
        P("case"),
        P(),
        P("bus", None),
        P("bus"),
        P("bus"),
        P("bus"),
        P("bus"),
    )
    out_specs = (P("bus", "case"), P("bus", "case"), P("bus"))
    return jax.shard_map(
        per_device, mesh=mesh, in_specs=in_specs, out_specs=out_specs, check_vma=False
    )
```

```python
import functools

import jax
import jax.numpy as jnp
from jax import lax
from jax.experimental import pallas as pl
from jax.experimental.pallas import tpu as pltpu
from jax.sharding import PartitionSpec as P

RIM = 256
TILE = 256
F32 = jnp.float32
BF16 = jnp.bfloat16


def split_hi_lo(value):
    hi = value.astype(BF16)
    return hi, (value - hi.astype(F32)).astype(BF16)


def two_pass(hi, lo, rhs):
    return jnp.dot(hi, rhs, preferred_element_type=F32) + jnp.dot(
        lo, rhs, preferred_element_type=F32
    )


def in_hbm(*arrays):
    return [pltpu.with_memory_space_constraint(x, pltpu.HBM) for x in arrays]


def stage_kernel(
    half, z_hbm, lists_hbm, fault_hbm, switch_hbm, send_ref, z_ref, pick_ref, lists, cases, sems
):
    rows = z_ref.shape[0]
    tiles = rows // RIM
    piece = send_ref.shape[0]
    my_bus, my_case = lax.axis_index("bus"), lax.axis_index("case")
    down = my_case // half
    rim = (1 - down) * (tiles - 1)

    def load(t):
        span = pl.ds(pl.multiple_of(lax.rem(rim + t, tiles) * RIM, RIM), RIM)
        return pltpu.make_async_copy(z_hbm.at[span], z_ref.at[span], sems.at[t])

    loads = [load(t) for t in range(tiles)]
    small = [
        pltpu.make_async_copy(lists_hbm.at[my_bus], lists, sems.at[tiles]),
        pltpu.make_async_copy(fault_hbm, cases.at[pl.ds(0, 1)], sems.at[tiles + 1]),
        pltpu.make_async_copy(switch_hbm, cases.at[pl.ds(8, 2)], sems.at[tiles + 2]),
    ]
    loads[0].start()
    for copy in small + loads[1:]:
        copy.start()
    for copy in small[:1] + loads[:1]:
        copy.wait()
    base = (my_case % half) * piece
    for i in range(piece):
        send_ref[pl.ds(i, 1), :] = z_ref[pl.ds(lists[1 - down, base + i], 1), :]
    for copy in small[1:]:
        copy.wait()
    fill_picks(cases[0:1, :], cases[8:10, :], pick_ref)
    for copy in loads[1:]:
        copy.wait()


def stage(z_columns, boundary_send, fault, switch, n_case):
    rows, cols = z_columns.shape
    half = n_case // 2
    count = fault.shape[1]
    hbm = pl.BlockSpec(memory_space=pltpu.HBM)
    vmem = pl.BlockSpec(memory_space=pltpu.VMEM)
    return pl.pallas_call(
        functools.partial(stage_kernel, half),
        in_specs=[hbm] * 4,
        out_specs=[vmem] * 3,
        out_shape=[
            pltpu.VMEM((boundary_send.shape[2] // half, cols), F32),
            pltpu.VMEM((rows, cols), F32),
            pltpu.VMEM((cols, 2 * count), BF16),
        ],
        scratch_shapes=[
            pltpu.SMEM(boundary_send.shape[1:], jnp.int32),
            pltpu.VMEM((16, count), jnp.int32),
            pltpu.SemaphoreType.DMA((rows // RIM + 3,)),
        ],
        compiler_params=pltpu.CompilerParams(vmem_limit_bytes=4 * 2**20),
        name="stage",
    )(*in_hbm(z_columns, boundary_send, fault, switch))


def fill_picks(f, ab, pick):
    cols, count = pick.shape[0], f.shape[1]
    a, b = ab[0:1, :], ab[1:2, :]
    for t in range(cols // TILE):
        k = lax.broadcasted_iota(jnp.int32, (TILE, count), 0) + t * TILE
        span = pl.ds(t * TILE, TILE)
        pick[span, :count] = jnp.where(k == f, 1.0, 0.0).astype(BF16)
        pick[span, count:] = jnp.where(k == a, 1.0, jnp.where(k == b, -1.0, 0.0)).astype(BF16)


def columns_kernel(z_ref, pick, fault_ref, switch_ref, resident_ref, fd_ref, g_ref):
    rows, cols = z_ref.shape
    cases = fault_ref.shape[1]
    f, a, b = fault_ref[...], switch_ref[0:1, :], switch_ref[1:2, :]
    resident = resident_ref[...] - lax.axis_index("bus") * rows
    g1 = jnp.zeros((1, cases), F32)
    g2 = jnp.zeros((1, cases), F32)
    g3 = jnp.zeros((1, cases), F32)
    for t in range(rows // TILE):
        span = pl.ds(t * TILE, TILE)
        row = lax.broadcasted_iota(jnp.int32, (TILE, cols), 0) + t * TILE
        k = lax.broadcasted_iota(jnp.int32, (TILE, cols), 1)
        owner = jnp.max(jnp.where(row == resident, k, -1), axis=1, keepdims=True)
        hi, lo = split_hi_lo(z_ref[span, :])
        fd = two_pass(hi, lo, pick[...])
        fd_ref[span, :] = fd
        fault, diff = fd[:, :cases], fd[:, cases:]
        at_f = owner == f
        g3 += jnp.sum(jnp.where(at_f, fault, 0.0), axis=0, keepdims=True)
        g2 += jnp.sum(jnp.where(at_f, diff, 0.0), axis=0, keepdims=True)
        g1 += jnp.sum(
            jnp.where(owner == a, diff, jnp.where(owner == b, -diff, 0.0)), axis=0, keepdims=True
        )
    g_ref[...] = jnp.concatenate([g1, g2, g3, jnp.zeros((g_ref.shape[0] - 3, cases), F32)])


def pick_columns(z, pick, fault, switch, resident):
    count = fault.shape[1]
    vmem = pl.BlockSpec(memory_space=pltpu.VMEM)
    return pl.pallas_call(
        columns_kernel,
        in_specs=[vmem] * 5,
        out_specs=[vmem, vmem],
        out_shape=[
            pltpu.VMEM((z.shape[0], 2 * count), F32),
            pltpu.VMEM((4, count), F32),
        ],
        compiler_params=pltpu.CompilerParams(vmem_limit_bytes=16 * 2**20),
        name="pick_columns",
    )(z, pick, fault, switch, resident)


def curve_constants(curve):
    half_power = jnp.where(curve == 0, 0.01, jnp.where(curve == 1, 0.5, 1.0)).astype(F32)
    factor = jnp.where(curve == 0, 0.14, jnp.where(curve == 1, 13.5, 80.0)).astype(F32)
    return half_power, factor


def pack_kernel(ends_ref, x_ref, pickup_ref, tds_ref, curve_ref, own, other, packed_ref, par_ref, sems):
    size = own.shape[0]
    loads = [
        pltpu.make_async_copy(own, packed_ref.at[pl.ds(0, size)], sems.at[0]),
        pltpu.make_async_copy(other, packed_ref.at[pl.ds(size, size)], sems.at[1]),
    ]
    for load in loads:
        load.start()
    ends = ends_ref[...].astype(F32)
    gain = 1.0 / (x_ref[...] * pickup_ref[...])
    half_power, factor = curve_constants(curve_ref[...])
    rate = 1.0 / (factor * tds_ref[...])
    par = jnp.concatenate([ends, gain, half_power, rate, jnp.zeros((3, ends.shape[1]), F32)])
    for c in range(0, ends.shape[1], 128):
        par_ref[pl.ds(c, 128), :] = par[:, c : c + 128].T
    for load in loads:
        load.wait()


def pack(branch_rows, own, other):
    vmem = pl.BlockSpec(memory_space=pltpu.VMEM)
    anywhere = pl.BlockSpec(memory_space=pl.ANY)
    return pl.pallas_call(
        pack_kernel,
        in_specs=[vmem] * len(branch_rows) + [anywhere] * 2,
        out_specs=[vmem, vmem],
        out_shape=[
            pltpu.VMEM((2 * own.shape[0], own.shape[1]), F32),
            pltpu.VMEM((branch_rows[0].shape[1], 8), F32),
        ],
        scratch_shapes=[pltpu.SemaphoreType.DMA((2,))],
        compiler_params=pltpu.CompilerParams(vmem_limit_bytes=4 * 2**20),
        name="pack",
    )(*branch_rows, own, other)


def boundary_kernel(order, fault_ref, switch_ref, *refs):
    n = len(order) // 2
    pairs = refs[:n]
    out_ref, pick, zb, sems = refs[n:]
    size = pairs[0].shape[0] // 2
    my_case = lax.axis_index("case")
    loads = []
    for i, mask in enumerate(order):
        first = pl.multiple_of((my_case ^ mask) * size, size)
        piece = pairs[i // 2].at[pl.ds(i % 2 * size, size)]
        loads.append(pltpu.make_async_copy(piece, zb.at[pl.ds(first, size)], sems.at[i]))
        loads[-1].start()
    fill_picks(fault_ref[...], switch_ref[...], pick)
    for load in loads:
        load.wait()
    hi, lo = split_hi_lo(zb[...])
    out_ref[...] = two_pass(hi, lo, pick[...])


def boundary_columns(order, fault, switch, pairs):
    cols = pairs[0].shape[1]
    total = sum(pair.shape[0] for pair in pairs)
    count = fault.shape[1]
    vmem = pl.BlockSpec(memory_space=pltpu.VMEM)
    anywhere = pl.BlockSpec(memory_space=pl.ANY)
    return pl.pallas_call(
        functools.partial(boundary_kernel, order),
        in_specs=[vmem] * 2 + [anywhere] * len(pairs),
        out_specs=vmem,
        out_shape=pltpu.VMEM((total, 2 * count), F32),
        scratch_shapes=[
            pltpu.VMEM((cols, 2 * count), BF16),
            pltpu.VMEM((total, cols), F32),
            pltpu.SemaphoreType.DMA((len(order),)),
        ],
        compiler_params=pltpu.CompilerParams(vmem_limit_bytes=16 * 2**20),
        cost_estimate=pl.CostEstimate(
            flops=8 * total * cols * count, bytes_accessed=8 * total * cols, transcendentals=0
        ),
        name="boundary_columns",
    )(fault, switch, *pairs)


def relay_of_square(square, power, rate):
    return jnp.maximum(jnp.exp2(power * jnp.log2(square + 1e-4)) - 1.0, 0.0) * rate


def branch_kernel(
    early,
    g_ref,
    tie_ref,
    fault_ref,
    par_ref,
    fd_ref,
    edge_ref,
    volt_hbm,
    relay_hbm,
    square_ref,
    worst_ref,
    vbuf,
    rbuf,
    uh,
    ul,
    vsem,
    rsem,
):
    rows, cases = vbuf.shape
    branches = par_ref.shape[0]
    ext = uh.shape[0]
    g1, g2, g3 = g_ref[0:1, :], g_ref[1:2, :], g_ref[2:3, :]
    ratio = g2 / (tie_ref[...] + g1)
    amps = 1.0 / (g3 - g2 * ratio + fault_ref[...])

    def sag_of(fd, span):
        sag = (fd[:, :cases] - fd[:, cases:] * ratio) * amps
        uh[span, :], ul[span, :] = split_hi_lo(sag)
        return sag

    sag_of(edge_ref[...], pl.ds(rows, ext - rows))
    copies = []
    for t in range(rows // TILE):
        span = pl.ds(t * TILE, TILE)
        vbuf[span, :] = 1.0 - sag_of(fd_ref[span, :], span)
        copies.append(pltpu.make_async_copy(vbuf.at[span], volt_hbm.at[span], vsem.at[t]))
        copies[-1].start()
    for t in range(branches // TILE):
        span = pl.ds(t * TILE, TILE)
        par = par_ref[span, :]
        bus = lax.broadcasted_iota(jnp.int32, (TILE, ext), 1).astype(F32)
        ends = jnp.where(
            bus == par[:, 1:2], 1.0, jnp.where(bus == par[:, 0:1], -1.0, 0.0)
        ).astype(BF16)
        drop = jnp.dot(ends, uh[...], preferred_element_type=F32) + jnp.dot(
            ends, ul[...], preferred_element_type=F32
        )
        scaled = drop * par[:, 2:3]
        square = scaled * scaled
        if t * TILE < early:
            rbuf[span, :] = relay_of_square(square, par[:, 3:4], par[:, 4:5])
            copies.append(pltpu.make_async_copy(rbuf.at[span], relay_hbm.at[span], rsem.at[t]))
            copies[-1].start()
        else:
            square_ref[pl.ds(t * TILE - early, TILE), :] = square
        largest = square[:, :128]
        for c in range(128, cases, 128):
            largest = jnp.maximum(largest, square[:, c : c + 128])
        for h in range(TILE // 128):
            worst_ref[pl.ds(t * (TILE // 128) + h, 1), :] = jnp.max(
                largest[h * 128 : (h + 1) * 128, :].T, axis=0, keepdims=True
            )
    for copy in copies:
        copy.wait()


def screen_branches(g, tie_x, fault_z, par, fd, edge, early):
    count = tie_x.shape[1]
    rows = fd.shape[0]
    branches = par.shape[0]
    ext = rows + edge.shape[0]
    vmem = pl.BlockSpec(memory_space=pltpu.VMEM)
    hbm = pl.BlockSpec(memory_space=pltpu.HBM)
    return pl.pallas_call(
        functools.partial(branch_kernel, early),
        in_specs=[vmem] * 6,
        out_specs=[hbm, hbm, vmem, vmem],
        out_shape=[
            jax.ShapeDtypeStruct((rows, count), F32),
            jax.ShapeDtypeStruct((branches, count), F32),
            pltpu.VMEM((branches - early, count), F32),
            pltpu.VMEM((branches // 128, 128), F32),
        ],
        scratch_shapes=[
            pltpu.VMEM((rows, count), F32),
            pltpu.VMEM((early, count), F32),
            pltpu.VMEM((ext, count), BF16),
            pltpu.VMEM((ext, count), BF16),
            pltpu.SemaphoreType.DMA((rows // TILE,)),
            pltpu.SemaphoreType.DMA((branches // TILE,)),
        ],
        compiler_params=pltpu.CompilerParams(vmem_limit_bytes=32 * 2**20),
        name="screen_branches",
    )(g, tie_x, fault_z, par, fd, edge)


def late_kernel(early, square_ref, par_ref, relay_in, relay_hbm, rbuf, sems):
    copies = []
    for t in range(square_ref.shape[0] // TILE):
        span = pl.ds(t * TILE, TILE)
        par = par_ref[pl.ds(early + t * TILE, TILE), :]
        rbuf[span, :] = relay_of_square(square_ref[span, :], par[:, 3:4], par[:, 4:5])
        copies.append(
            pltpu.make_async_copy(
                rbuf.at[span], relay_hbm.at[pl.ds(early + t * TILE, TILE)], sems.at[t]
            )
        )
        copies[-1].start()
    for copy in copies:
        copy.wait()


def late_relays(square, par, relay_rate, early):
    vmem = pl.BlockSpec(memory_space=pltpu.VMEM)
    hbm = pl.BlockSpec(memory_space=pltpu.HBM)
    return pl.pallas_call(
        functools.partial(late_kernel, early),
        in_specs=[vmem, vmem, hbm],
        out_specs=hbm,
        out_shape=jax.ShapeDtypeStruct(relay_rate.shape, F32),
        input_output_aliases={2: 0},
        scratch_shapes=[
            pltpu.VMEM(square.shape, F32),
            pltpu.SemaphoreType.DMA((square.shape[0] // TILE,)),
        ],
        compiler_params=pltpu.CompilerParams(vmem_limit_bytes=8 * 2**20),
        cost_estimate=pl.CostEstimate(
            flops=8 * square.size, bytes_accessed=8 * square.size, transcendentals=2 * square.size
        ),
        name="late_relays",
    )(square, par, relay_rate)


def per_device(
    z_columns,
    resident_bus,
    fault_col,
    switch_cols,
    tie_x,
    fault_z,
    boundary_send,
    branch_ends,
    branch_x,
    pickup,
    tds,
    curve,
):
    n_bus, n_case = lax.axis_size("bus"), lax.axis_size("case")
    half = n_case // 2
    fault, switch = fault_col[None], switch_cols.T
    send, z, pick = stage(z_columns, boundary_send, fault, switch, n_case)
    pairs = []
    for s in range(n_bus):
        for c in range(n_case):
            to = s + 1 if c < half else s - 1
            if 0 <= to < n_bus:
                pairs.append((s * n_case + c, to * n_case + c))
    own = lax.ppermute(send, ("bus", "case"), pairs)

    fd, g = pick_columns(z, pick, fault, switch, resident_bus[None])
    g, own = lax.optimization_barrier((g, own))

    def add_over_bus(g, bit):
        return g + lax.ppermute(g, "bus", [(i, i ^ bit) for i in range(n_bus)])

    other = lax.ppermute(own, "case", [(i, i ^ half) for i in range(n_case)])
    bit = 1
    while bit < n_bus // 2:
        g = add_over_bus(g, bit)
        bit *= 2
    g, other = lax.optimization_barrier((g, other))
    branch_rows = [branch_ends.T, branch_x[None], pickup[None], tds[None], curve[None]]
    packed, par = pack(branch_rows, own, other)
    packs = [packed]
    order = [0, half]
    bit = half // 2
    while bit:
        swap = [(i, i ^ bit) for i in range(n_case)]
        packs = packs + [lax.ppermute(x, "case", swap) for x in packs]
        order = order + [m ^ bit for m in order]
        bit //= 2
    g = add_over_bus(g, n_bus // 2)
    edge = boundary_columns(order, fault, switch, packs)
    early = par.shape[0] * 2 // 3 // TILE * TILE
    voltage, relay_rate, square, worst = screen_branches(
        g, tie_x[None], fault_z[None], par, fd, edge, early
    )
    bit = 1
    while bit < n_case:
        other = lax.ppermute(worst, "case", [(i, i ^ bit) for i in range(n_case)])
        worst = jnp.maximum(worst, other)
        bit *= 2
    relay_rate = late_relays(square, par, relay_rate, early)
    half_power, factor = curve_constants(curve)
    worst_rate = relay_of_square(worst.reshape(-1), half_power, 1.0 / (factor * tds))
    return (voltage, relay_rate, worst_rate)


def solution(mesh):
    in_specs = (
        P("bus", None),
        P(),
        P("case"),
        P("case", None),
        P("case"),
        P("case"),
        P(),
        P("bus", None),
        P("bus"),
        P("bus"),
        P("bus"),
        P("bus"),
    )
    out_specs = (P("bus", "case"), P("bus", "case"), P("bus"))
    return jax.shard_map(
        per_device, mesh=mesh, in_specs=in_specs, out_specs=out_specs, check_vma=False
    )
```

```python
import functools

import jax
import jax.numpy as jnp
from jax import lax
from jax.experimental import pallas as pl
from jax.experimental.pallas import tpu as pltpu
from jax.sharding import PartitionSpec as P

TILE = 256
STAGED = 2
F32 = jnp.float32
BF16 = jnp.bfloat16


def split_hi_lo(value):
    hi = value.astype(BF16)
    return hi, (value - hi.astype(F32)).astype(BF16)


def two_pass(hi, lo, rhs):
    return jnp.dot(hi, rhs, preferred_element_type=F32) + jnp.dot(
        lo, rhs, preferred_element_type=F32
    )


def in_hbm(*arrays):
    return [pltpu.with_memory_space_constraint(x, pltpu.HBM) for x in arrays]


def rim_tile(half, tiles):
    return (1 - lax.axis_index("case") // half) * (tiles - 1)


def tile_span(t, tiles):
    return pl.ds(pl.multiple_of(lax.rem(t, tiles) * TILE, TILE), TILE)


def stage_kernel(
    half, z_hbm, lists_hbm, fault_hbm, switch_hbm, send_ref, z_ref, pick_ref, lists, cases, sems
):
    tiles = z_hbm.shape[0] // TILE
    piece = send_ref.shape[0]
    my_bus, my_case = lax.axis_index("bus"), lax.axis_index("case")
    rim = rim_tile(half, tiles)
    loads = [
        pltpu.make_async_copy(fault_hbm, cases.at[pl.ds(0, 1)], sems.at[0]),
        pltpu.make_async_copy(switch_hbm, cases.at[pl.ds(8, 2)], sems.at[1]),
        pltpu.make_async_copy(lists_hbm.at[my_bus], lists, sems.at[2]),
    ]
    for t in range(z_ref.shape[0] // TILE):
        target = z_ref.at[pl.ds(t * TILE, TILE)]
        source = z_hbm.at[tile_span(rim + t, tiles)]
        loads.append(pltpu.make_async_copy(source, target, sems.at[3 + t]))
    for load in loads:
        load.start()
    for load in loads[:2]:
        load.wait()
    fill_picks(cases[0:1, :], cases[8:10, :], pick_ref)
    for load in loads[2:4]:
        load.wait()
    down = my_case // half
    base = (my_case % half) * piece
    first = rim * TILE
    for i in range(piece):
        send_ref[pl.ds(i, 1), :] = z_ref[pl.ds(lists[1 - down, base + i] - first, 1), :]
    for load in loads[4:]:
        load.wait()


def stage(z_columns, boundary_send, fault, switch, n_case):
    cols = z_columns.shape[1]
    half = n_case // 2
    count = fault.shape[1]
    return pl.pallas_call(
        functools.partial(stage_kernel, half),
        in_specs=[pl.BlockSpec(memory_space=pltpu.HBM)] * 4,
        out_specs=[pl.BlockSpec(memory_space=pltpu.VMEM)] * 3,
        out_shape=[
            pltpu.VMEM((boundary_send.shape[2] // half, cols), F32),
            pltpu.VMEM((STAGED * TILE, cols), F32),
            pltpu.VMEM((cols, 2 * count), BF16),
        ],
        scratch_shapes=[
            pltpu.SMEM(boundary_send.shape[1:], jnp.int32),
            pltpu.VMEM((16, count), jnp.int32),
            pltpu.SemaphoreType.DMA((STAGED + 3,)),
        ],
        compiler_params=pltpu.CompilerParams(vmem_limit_bytes=4 * 2**20),
        name="stage",
    )(*in_hbm(z_columns, boundary_send, fault, switch))


def fill_picks(f, ab, pick):
    cols, count = pick.shape[0], f.shape[1]
    a, b = ab[0:1, :], ab[1:2, :]
    for t in range(cols // TILE):
        k = lax.broadcasted_iota(jnp.int32, (TILE, count), 0) + t * TILE
        span = pl.ds(t * TILE, TILE)
        pick[span, :count] = jnp.where(k == f, 1.0, 0.0).astype(BF16)
        pick[span, count:] = jnp.where(k == a, 1.0, jnp.where(k == b, -1.0, 0.0)).astype(BF16)


def columns_kernel(
    half,
    z_ref,
    pick,
    fault_ref,
    switch_ref,
    resident_ref,
    z_hbm,
    ends_hbm,
    x_hbm,
    pickup_hbm,
    tds_hbm,
    curve_hbm,
    fd_ref,
    g_ref,
    par_ref,
    fd_hi,
    fd_lo,
    later,
    ends,
    floats,
    curves,
    sems,
):
    rows, cols = z_hbm.shape
    cases = fault_ref.shape[1]
    tiles = rows // TILE
    rim = rim_tile(half, tiles)
    loads = []
    for t in range(STAGED, tiles):
        target = later.at[pl.ds((t - STAGED) * TILE, TILE)]
        source = z_hbm.at[tile_span(rim + t, tiles)]
        loads.append(pltpu.make_async_copy(source, target, sems.at[t]))
    small = [
        pltpu.make_async_copy(source, target, sems.at[tiles + i])
        for i, (source, target) in enumerate(
            [
                (ends_hbm, ends),
                (x_hbm, floats.at[0]),
                (pickup_hbm, floats.at[1]),
                (tds_hbm, floats.at[2]),
                (curve_hbm, curves),
            ]
        )
    ]
    for load in loads + small:
        load.start()
    f, a, b = fault_ref[...], switch_ref[0:1, :], switch_ref[1:2, :]
    resident = resident_ref[...] - lax.axis_index("bus") * rows
    g1 = jnp.zeros((1, cases), F32)
    g2 = jnp.zeros((1, cases), F32)
    g3 = jnp.zeros((1, cases), F32)
    k = lax.broadcasted_iota(jnp.int32, (TILE, cols), 1)
    for t in range(tiles + 1):
        if t == STAGED:
            for load in loads + small:
                load.wait()
        if t < tiles:
            if t < STAGED:
                z = z_ref[pl.ds(t * TILE, TILE), :]
            else:
                z = later[pl.ds((t - STAGED) * TILE, TILE), :]
            hi, lo = split_hi_lo(z)
            fd_ref[pl.ds(t * TILE, TILE), :] = two_pass(hi, lo, pick[...])
        if t == STAGED:
            gain = 1.0 / (floats[0] * floats[1])
            half_power, factor = curve_constants(curves[...])
            rate = 1.0 / (factor * floats[2])
            for c in range(gain.shape[0]):
                line = pl.ds(c * 128, 128)
                lines = [ends[:, line].astype(F32)]
                lines += [x[c : c + 1] for x in (gain, half_power, rate)]
                par_ref[line, :] = jnp.concatenate(lines + [jnp.zeros((3, 128), F32)]).T
        if t > 0:
            span = pl.ds((t - 1) * TILE, TILE)
            first = tile_span(rim + t - 1, tiles).start
            row = lax.broadcasted_iota(jnp.int32, (TILE, cols), 0) + first
            owner = jnp.max(jnp.where(row == resident, k, -1), axis=1, keepdims=True)
            fd_hi[span, :], fd_lo[span, :] = split_hi_lo(fd_ref[span, :])
            fault, diff = fd_ref[span, :cases], fd_ref[span, cases:]
            at_f = owner == f
            g3 += jnp.sum(jnp.where(at_f, fault, 0.0), axis=0, keepdims=True)
            g2 += jnp.sum(jnp.where(at_f, diff, 0.0), axis=0, keepdims=True)
            g1 += jnp.sum(
                jnp.where(owner == a, diff, jnp.where(owner == b, -diff, 0.0)),
                axis=0,
                keepdims=True,
            )
    g_ref[...] = jnp.concatenate([g1, g2, g3, jnp.zeros((g_ref.shape[0] - 3, cases), F32)])


def pick_columns(z, pick, fault, switch, resident, z_columns, ends, values, curve, n_case):
    rows, cols = z_columns.shape
    count = fault.shape[1]
    lines = curve.shape[0]
    vmem = pl.BlockSpec(memory_space=pltpu.VMEM)
    return pl.pallas_call(
        functools.partial(columns_kernel, n_case // 2),
        in_specs=[vmem] * 5 + [pl.BlockSpec(memory_space=pltpu.HBM)] * 6,
        out_specs=[vmem] * 5,
        out_shape=[
            pltpu.VMEM((rows, 2 * count), F32),
            pltpu.VMEM((4, count), F32),
            pltpu.VMEM((lines * 128, 8), F32),
            pltpu.VMEM((rows, 2 * count), BF16),
            pltpu.VMEM((rows, 2 * count), BF16),
        ],
        scratch_shapes=[
            pltpu.VMEM((rows - STAGED * TILE, cols), F32),
            pltpu.VMEM(ends.shape, jnp.int32),
            pltpu.VMEM((3, lines, 128), F32),
            pltpu.VMEM((lines, 128), jnp.int32),
            pltpu.SemaphoreType.DMA((rows // TILE + 5,)),
        ],
        compiler_params=pltpu.CompilerParams(vmem_limit_bytes=20 * 2**20),
        name="pick_columns",
    )(z, pick, fault, switch, resident, *in_hbm(z_columns, ends, *values, curve))


def curve_constants(curve):
    half_power = jnp.where(curve == 0, 0.01, jnp.where(curve == 1, 0.5, 1.0)).astype(F32)
    factor = jnp.where(curve == 0, 0.14, jnp.where(curve == 1, 13.5, 80.0)).astype(F32)
    return half_power, factor


def incidence(bus, par):
    return jnp.where(bus == par[:, 1:2], 1.0, jnp.where(bus == par[:, 0:1], -1.0, 0.0)).astype(BF16)


def advance_kernel(half, start, fd_hi, fd_lo, par_ref, out_ref):
    rows = fd_hi.shape[0]
    count = out_ref.shape[0]
    bus = lax.broadcasted_iota(jnp.int32, (count, rows), 1)
    bus = bus + rim_tile(half, rows // TILE) * TILE
    bus = jnp.where(bus >= rows, bus - rows, bus).astype(F32)
    ends = incidence(bus, par_ref[pl.ds(start, count), :])
    out_ref[...] = jnp.dot(ends, fd_hi[...], preferred_element_type=F32) + jnp.dot(
        ends, fd_lo[...], preferred_element_type=F32
    )


def advance(fd_parts, par, start, count, n_case):
    rows, width = fd_parts[0].shape
    vmem = pl.BlockSpec(memory_space=pltpu.VMEM)
    return pl.pallas_call(
        functools.partial(advance_kernel, n_case // 2, start),
        in_specs=[vmem] * 3,
        out_specs=vmem,
        out_shape=pltpu.VMEM((count, width), F32),
        compiler_params=pltpu.CompilerParams(vmem_limit_bytes=8 * 2**20),
        cost_estimate=pl.CostEstimate(
            flops=4 * count * rows * width, bytes_accessed=8 * count * width, transcendentals=0
        ),
        name="advance",
    )(*fd_parts, par)


def boundary_kernel(order, pick, *refs):
    pieces = refs[: len(order)]
    out_ref, hi, lo = refs[len(order) :]
    my_case = lax.axis_index("case")
    for mask, piece in zip(order, pieces):
        size = piece.shape[0]
        span = pl.ds(pl.multiple_of((my_case ^ mask) * size, size), size)
        hi[span, :], lo[span, :] = split_hi_lo(piece[...])
    out_ref[...] = two_pass(hi[...], lo[...], pick[...])


def boundary_columns(order, pick, pieces):
    cols, width = pick.shape
    total = sum(piece.shape[0] for piece in pieces)
    vmem = pl.BlockSpec(memory_space=pltpu.VMEM)
    return pl.pallas_call(
        functools.partial(boundary_kernel, order),
        in_specs=[vmem] * (1 + len(pieces)),
        out_specs=vmem,
        out_shape=pltpu.VMEM((total, width), F32),
        scratch_shapes=[pltpu.VMEM((total, cols), BF16)] * 2,
        compiler_params=pltpu.CompilerParams(vmem_limit_bytes=8 * 2**20),
        cost_estimate=pl.CostEstimate(
            flops=4 * total * cols * width, bytes_accessed=8 * total * cols, transcendentals=0
        ),
        name="boundary_columns",
    )(pick, *pieces)


def relay_of_square(square, power, rate):
    return jnp.maximum(jnp.exp2(power * jnp.log2(square + 1e-4)) - 1.0, 0.0) * rate


def branch_kernel(half, n_ahead, g_ref, far_ref, tie_ref, fault_ref, par_ref, fd_ref, edge_ref, *refs):
    ahead = refs[:n_ahead]
    volt_hbm, relay_hbm, square_ref, worst_ref, vbuf, rbuf, uh, ul, vsem, rsem = refs[n_ahead:]
    rows, cases = vbuf.shape
    branches = par_ref.shape[0]
    early = square_ref.shape[0]
    ext = uh.shape[0]
    g = g_ref[...] + far_ref[...]
    g1, g2, g3 = g[0:1], g[1:2], g[2:3]
    ratio = g2 / (tie_ref[...] + g1)
    amps = 1.0 / (g3 - g2 * ratio + fault_ref[...])

    def sag_of(fd):
        return (fd[:, :cases] - fd[:, cases:] * ratio) * amps

    edge = pl.ds(rows, ext - rows)
    uh[edge, :], ul[edge, :] = split_hi_lo(sag_of(edge_ref[...]))
    tiles = rows // TILE
    rim = rim_tile(half, tiles)
    for t in range(tiles):
        span = tile_span(rim + t, tiles)
        sag = sag_of(fd_ref[pl.ds(t * TILE, TILE), :])
        vbuf[span, :] = 1.0 - sag
        uh[span, :], ul[span, :] = split_hi_lo(sag)
    copies = [pltpu.make_async_copy(vbuf, volt_hbm, vsem)]
    copies[0].start()

    def drops(par, first):
        count = par.shape[0]
        bus = lax.broadcasted_iota(jnp.int32, (count, ext - first), 1) + first
        ends = incidence(bus.astype(F32), par)
        span = pl.ds(first, ext - first)
        return jnp.dot(ends, uh[span, :], preferred_element_type=F32) + jnp.dot(
            ends, ul[span, :], preferred_element_type=F32
        )

    def square_of(drop, par, start):
        scaled = drop * par[:, 2:3]
        square = scaled * scaled
        largest = square[:, :128]
        for c in range(128, cases, 128):
            largest = jnp.maximum(largest, square[:, c : c + 128])
        for h in range(par.shape[0] // 128):
            worst_ref[pl.ds(start // 128 + h, 1), :] = jnp.max(
                largest[h * 128 : (h + 1) * 128, :].T, axis=0, keepdims=True
            )
        return square

    start = 0
    ready = []
    for part in ahead:
        ready.append((part, start))
        start += part.shape[0]
    for t in range((branches - early) // TILE):
        start = early + t * TILE
        par = par_ref[pl.ds(start, TILE), :]
        square = square_of(drops(par, 0), par, start)
        span = pl.ds(t * TILE, TILE)
        rbuf[span, :] = relay_of_square(square, par[:, 3:4], par[:, 4:5])
        if t < len(ready):
            part, start = ready[t]
            count = part.shape[0]
            par = par_ref[pl.ds(start, count), :]
            drop = sag_of(part[...]) + drops(par, rows)
            square_ref[pl.ds(start, count), :] = square_of(drop, par, start)
        target = relay_hbm.at[pl.ds(early + t * TILE, TILE)]
        copies.append(pltpu.make_async_copy(rbuf.at[span], target, rsem.at[t]))
        copies[-1].start()
    for copy in copies:
        copy.wait()


def screen_branches(g, g_far, tie_x, fault_z, par, fd, edge, ahead, n_case):
    count = tie_x.shape[1]
    rows = fd.shape[0]
    branches = par.shape[0]
    early = sum(part.shape[0] for part in ahead)
    ext = rows + edge.shape[0]
    vmem = pl.BlockSpec(memory_space=pltpu.VMEM)
    hbm = pl.BlockSpec(memory_space=pltpu.HBM)
    return pl.pallas_call(
        functools.partial(branch_kernel, n_case // 2, len(ahead)),
        in_specs=[vmem] * (7 + len(ahead)),
        out_specs=[hbm, hbm, vmem, vmem],
        out_shape=[
            jax.ShapeDtypeStruct((rows, count), F32),
            jax.ShapeDtypeStruct((branches, count), F32),
            pltpu.VMEM((early, count), F32),
            pltpu.VMEM((branches // 128, 128), F32),
        ],
        scratch_shapes=[
            pltpu.VMEM((rows, count), F32),
            pltpu.VMEM((branches - early, count), F32),
            pltpu.VMEM((ext, count), BF16),
            pltpu.VMEM((ext, count), BF16),
            pltpu.SemaphoreType.DMA,
            pltpu.SemaphoreType.DMA((branches // TILE,)),
        ],
        compiler_params=pltpu.CompilerParams(vmem_limit_bytes=24 * 2**20),
        name="screen_branches",
    )(g, g_far, tie_x, fault_z, par, fd, edge, *ahead)


def late_kernel(square_ref, par_ref, relay_in, relay_hbm, rbuf, sems):
    copies = []
    for t in range(square_ref.shape[0] // TILE):
        span = pl.ds(t * TILE, TILE)
        par = par_ref[span, :]
        rbuf[span, :] = relay_of_square(square_ref[span, :], par[:, 3:4], par[:, 4:5])
        copies.append(pltpu.make_async_copy(rbuf.at[span], relay_hbm.at[span], sems.at[t]))
        copies[-1].start()
    for copy in copies:
        copy.wait()


def late_relays(square, par, relay_rate):
    vmem = pl.BlockSpec(memory_space=pltpu.VMEM)
    hbm = pl.BlockSpec(memory_space=pltpu.HBM)
    return pl.pallas_call(
        late_kernel,
        in_specs=[vmem, vmem, hbm],
        out_specs=hbm,
        out_shape=jax.ShapeDtypeStruct(relay_rate.shape, F32),
        input_output_aliases={2: 0},
        scratch_shapes=[
            pltpu.VMEM(square.shape, F32),
            pltpu.SemaphoreType.DMA((square.shape[0] // TILE,)),
        ],
        compiler_params=pltpu.CompilerParams(vmem_limit_bytes=8 * 2**20),
        cost_estimate=pl.CostEstimate(
            flops=8 * square.size, bytes_accessed=8 * square.size, transcendentals=2 * square.size
        ),
        name="late_relays",
    )(square, par, relay_rate)


def per_device(
    z_columns,
    resident_bus,
    fault_col,
    switch_cols,
    tie_x,
    fault_z,
    boundary_send,
    branch_ends,
    branch_x,
    pickup,
    tds,
    curve,
):
    n_bus, n_case = lax.axis_size("bus"), lax.axis_size("case")
    half = n_case // 2
    fault, switch = fault_col[None], switch_cols.T
    send, z, pick = stage(z_columns, boundary_send, fault, switch, n_case)
    pairs = []
    for s in range(n_bus):
        for c in range(n_case):
            to = s + 1 if c < half else s - 1
            if 0 <= to < n_bus:
                pairs.append((s * n_case + c, to * n_case + c))
    own = lax.ppermute(send, ("bus", "case"), pairs)

    by_lines = [x.reshape(-1, 128) for x in (branch_x, pickup, tds, curve)]
    fd, g, par, *fd_parts = pick_columns(
        z,
        pick,
        fault,
        switch,
        resident_bus[None],
        z_columns,
        branch_ends.T,
        by_lines[:3],
        by_lines[3],
        n_case,
    )

    def swap_over_bus(g, bit):
        return lax.ppermute(g, "bus", [(i, i ^ bit) for i in range(n_bus)])

    def after(first, *values):
        return lax.optimization_barrier((first, *values))[1:]

    (own,) = after(g, own)
    other = lax.ppermute(own, "case", [(i, i ^ half) for i in range(n_case)])
    ahead = []
    part = par.shape[0] // 4
    bit = 1
    while bit < n_bus // 2:
        far = swap_over_bus(g, bit)
        if len(ahead) < 2:
            ahead.append(advance(fd_parts, par, len(ahead) * part, part, n_case))
            (far,) = after(ahead[-1], far)
        g = g + far
        bit *= 2
    g_far = swap_over_bus(g, n_bus // 2)
    pieces, order = list(after(g, own, other)), [0, half]
    bit = half // 2
    while bit:
        swap = [(i, i ^ bit) for i in range(n_case)]
        pieces = pieces + [lax.ppermute(x, "case", swap) for x in pieces]
        order = order + [m ^ bit for m in order]
        bit //= 2
    edge = boundary_columns(order, pick, pieces)
    voltage, relay_rate, square, worst = screen_branches(
        g, g_far, tie_x[None], fault_z[None], par, fd, edge, ahead, n_case
    )
    others = [
        lax.ppermute(worst, "case", [(i, i ^ m) for i in range(n_case)])
        for m in range(n_case - 1, 0, -1)
    ]
    relay_rate = late_relays(square, par, relay_rate)
    half_power, factor = curve_constants(curve)
    worst = functools.reduce(jnp.maximum, others, worst).reshape(-1)
    worst_rate = relay_of_square(worst, half_power, 1.0 / (factor * tds))
    return (voltage, relay_rate, worst_rate)


def solution(mesh):
    in_specs = (
        P("bus", None),
        P(),
        P("case"),
        P("case", None),
        P("case"),
        P("case"),
        P(),
        P("bus", None),
        P("bus"),
        P("bus"),
        P("bus"),
        P("bus"),
    )
    out_specs = (P("bus", "case"), P("bus", "case"), P("bus"))
    return jax.shard_map(
        per_device, mesh=mesh, in_specs=in_specs, out_specs=out_specs, check_vma=False
    )
```

```python
import functools

import jax
import jax.numpy as jnp
from jax import lax
from jax.experimental import pallas as pl
from jax.experimental.pallas import tpu as pltpu
from jax.sharding import PartitionSpec as P

TILE = 256
STAGED = 2
F32 = jnp.float32
BF16 = jnp.bfloat16


def split_hi_lo(value):
    hi = value.astype(BF16)
    return hi, (value - hi.astype(F32)).astype(BF16)


def two_pass(hi, lo, rhs):
    return jnp.dot(hi, rhs, preferred_element_type=F32) + jnp.dot(
        lo, rhs, preferred_element_type=F32
    )


def in_hbm(*arrays):
    return [pltpu.with_memory_space_constraint(x, pltpu.HBM) for x in arrays]


def rim_tile(half, tiles):
    return (1 - lax.axis_index("case") // half) * (tiles - 1)


def tile_span(t, tiles):
    return pl.ds(pl.multiple_of(lax.rem(t, tiles) * TILE, TILE), TILE)


def stage_kernel(
    half, z_hbm, lists_hbm, fault_hbm, switch_hbm, send_ref, z_ref, pick_ref, lists, cases, sems
):
    tiles = z_hbm.shape[0] // TILE
    piece = send_ref.shape[0]
    my_bus, my_case = lax.axis_index("bus"), lax.axis_index("case")
    rim = rim_tile(half, tiles)
    loads = [
        pltpu.make_async_copy(fault_hbm, cases.at[pl.ds(0, 1)], sems.at[0]),
        pltpu.make_async_copy(switch_hbm, cases.at[pl.ds(8, 2)], sems.at[1]),
        pltpu.make_async_copy(lists_hbm.at[my_bus], lists, sems.at[2]),
    ]
    for t in range(z_ref.shape[0] // TILE):
        target = z_ref.at[pl.ds(t * TILE, TILE)]
        source = z_hbm.at[tile_span(rim + t, tiles)]
        loads.append(pltpu.make_async_copy(source, target, sems.at[3 + t]))
    for load in loads:
        load.start()
    for load in loads[:2]:
        load.wait()
    fill_picks(cases[0:1, :], cases[8:10, :], pick_ref)
    for load in loads[2:4]:
        load.wait()
    down = my_case // half
    base = (my_case % half) * piece
    first = rim * TILE
    for i in range(piece):
        send_ref[pl.ds(i, 1), :] = z_ref[pl.ds(lists[1 - down, base + i] - first, 1), :]
    for load in loads[4:]:
        load.wait()


def stage(z_columns, boundary_send, fault, switch, n_case):
    cols = z_columns.shape[1]
    half = n_case // 2
    count = fault.shape[1]
    return pl.pallas_call(
        functools.partial(stage_kernel, half),
        in_specs=[pl.BlockSpec(memory_space=pltpu.HBM)] * 4,
        out_specs=[pl.BlockSpec(memory_space=pltpu.VMEM)] * 3,
        out_shape=[
            pltpu.VMEM((boundary_send.shape[2] // half, cols), F32),
            pltpu.VMEM((STAGED * TILE, cols), F32),
            pltpu.VMEM((cols, 2 * count), BF16),
        ],
        scratch_shapes=[
            pltpu.SMEM(boundary_send.shape[1:], jnp.int32),
            pltpu.VMEM((16, count), jnp.int32),
            pltpu.SemaphoreType.DMA((STAGED + 3,)),
        ],
        compiler_params=pltpu.CompilerParams(vmem_limit_bytes=4 * 2**20),
        name="stage",
    )(*in_hbm(z_columns, boundary_send, fault, switch))


def fill_picks(f, ab, pick):
    cols, count = pick.shape[0], f.shape[1]
    a, b = ab[0:1, :], ab[1:2, :]
    for t in range(cols // TILE):
        k = lax.broadcasted_iota(jnp.int32, (TILE, count), 0) + t * TILE
        span = pl.ds(t * TILE, TILE)
        pick[span, :count] = jnp.where(k == f, 1.0, 0.0).astype(BF16)
        pick[span, count:] = jnp.where(k == a, 1.0, jnp.where(k == b, -1.0, 0.0)).astype(BF16)


def columns_kernel(
    half,
    z_ref,
    pick,
    fault_ref,
    switch_ref,
    resident_ref,
    z_hbm,
    ends_hbm,
    x_hbm,
    pickup_hbm,
    tds_hbm,
    curve_hbm,
    fd_ref,
    g_ref,
    par_ref,
    fd_hi,
    fd_lo,
    later,
    ends,
    floats,
    curves,
    sems,
):
    rows, cols = z_hbm.shape
    cases = fault_ref.shape[1]
    tiles = rows // TILE
    rim = rim_tile(half, tiles)
    loads = []
    for t in range(STAGED, tiles):
        target = later.at[pl.ds((t - STAGED) * TILE, TILE)]
        source = z_hbm.at[tile_span(rim + t, tiles)]
        loads.append(pltpu.make_async_copy(source, target, sems.at[t]))
    small = [
        pltpu.make_async_copy(source, target, sems.at[tiles + i])
        for i, (source, target) in enumerate(
            [
                (ends_hbm, ends),
                (x_hbm, floats.at[0]),
                (pickup_hbm, floats.at[1]),
                (tds_hbm, floats.at[2]),
                (curve_hbm, curves),
            ]
        )
    ]
    for load in loads + small:
        load.start()
    f, a, b = fault_ref[...], switch_ref[0:1, :], switch_ref[1:2, :]
    resident = resident_ref[...] - lax.axis_index("bus") * rows
    g1 = jnp.zeros((1, cases), F32)
    g2 = jnp.zeros((1, cases), F32)
    g3 = jnp.zeros((1, cases), F32)
    k = lax.broadcasted_iota(jnp.int32, (TILE, cols), 1)
    for t in range(tiles + 1):
        if t == STAGED:
            for load in loads + small:
                load.wait()
        if t < tiles:
            if t < STAGED:
                z = z_ref[pl.ds(t * TILE, TILE), :]
            else:
                z = later[pl.ds((t - STAGED) * TILE, TILE), :]
            hi, lo = split_hi_lo(z)
            fd_ref[pl.ds(t * TILE, TILE), :] = two_pass(hi, lo, pick[...])
        if t == STAGED:
            gain = 1.0 / (floats[0] * floats[1])
            half_power, factor = curve_constants(curves[...])
            rate = 1.0 / (factor * floats[2])
            for c in range(gain.shape[0]):
                line = pl.ds(c * 128, 128)
                lines = [ends[:, line].astype(F32)]
                lines += [x[c : c + 1] for x in (gain, half_power, rate)]
                par_ref[line, :] = jnp.concatenate(lines + [jnp.zeros((3, 128), F32)]).T
        if t > 0:
            span = pl.ds((t - 1) * TILE, TILE)
            first = tile_span(rim + t - 1, tiles).start
            row = lax.broadcasted_iota(jnp.int32, (TILE, cols), 0) + first
            owner = jnp.max(jnp.where(row == resident, k, -1), axis=1, keepdims=True)
            fd_hi[span, :], fd_lo[span, :] = split_hi_lo(fd_ref[span, :])
            fault, diff = fd_ref[span, :cases], fd_ref[span, cases:]
            at_f = owner == f
            g3 += jnp.sum(jnp.where(at_f, fault, 0.0), axis=0, keepdims=True)
            g2 += jnp.sum(jnp.where(at_f, diff, 0.0), axis=0, keepdims=True)
            g1 += jnp.sum(
                jnp.where(owner == a, diff, jnp.where(owner == b, -diff, 0.0)),
                axis=0,
                keepdims=True,
            )
    g_ref[...] = jnp.concatenate([g1, g2, g3, jnp.zeros((g_ref.shape[0] - 3, cases), F32)])


def pick_columns(z, pick, fault, switch, resident, z_columns, ends, values, curve, n_case):
    rows, cols = z_columns.shape
    count = fault.shape[1]
    lines = curve.shape[0]
    vmem = pl.BlockSpec(memory_space=pltpu.VMEM)
    return pl.pallas_call(
        functools.partial(columns_kernel, n_case // 2),
        in_specs=[vmem] * 5 + [pl.BlockSpec(memory_space=pltpu.HBM)] * 6,
        out_specs=[vmem] * 5,
        out_shape=[
            pltpu.VMEM((rows, 2 * count), F32),
            pltpu.VMEM((4, count), F32),
            pltpu.VMEM((lines * 128, 8), F32),
            pltpu.VMEM((rows, 2 * count), BF16),
            pltpu.VMEM((rows, 2 * count), BF16),
        ],
        scratch_shapes=[
            pltpu.VMEM((rows - STAGED * TILE, cols), F32),
            pltpu.VMEM(ends.shape, jnp.int32),
            pltpu.VMEM((3, lines, 128), F32),
            pltpu.VMEM((lines, 128), jnp.int32),
            pltpu.SemaphoreType.DMA((rows // TILE + 5,)),
        ],
        compiler_params=pltpu.CompilerParams(vmem_limit_bytes=20 * 2**20),
        name="pick_columns",
    )(z, pick, fault, switch, resident, *in_hbm(z_columns, ends, *values, curve))


def curve_constants(curve):
    half_power = jnp.where(curve == 0, 0.01, jnp.where(curve == 1, 0.5, 1.0)).astype(F32)
    factor = jnp.where(curve == 0, 0.14, jnp.where(curve == 1, 13.5, 80.0)).astype(F32)
    return half_power, factor


def incidence(bus, par):
    return jnp.where(bus == par[:, 1:2], 1.0, jnp.where(bus == par[:, 0:1], -1.0, 0.0)).astype(BF16)


def advance_kernel(half, start, fd_hi, fd_lo, par_ref, out_ref):
    rows = fd_hi.shape[0]
    count = out_ref.shape[0]
    bus = lax.broadcasted_iota(jnp.int32, (count, rows), 1)
    bus = bus + rim_tile(half, rows // TILE) * TILE
    bus = jnp.where(bus >= rows, bus - rows, bus).astype(F32)
    ends = incidence(bus, par_ref[pl.ds(start, count), :])
    out_ref[...] = jnp.dot(ends, fd_hi[...], preferred_element_type=F32) + jnp.dot(
        ends, fd_lo[...], preferred_element_type=F32
    )


def advance(fd_parts, par, start, count, n_case):
    rows, width = fd_parts[0].shape
    vmem = pl.BlockSpec(memory_space=pltpu.VMEM)
    return pl.pallas_call(
        functools.partial(advance_kernel, n_case // 2, start),
        in_specs=[vmem] * 3,
        out_specs=vmem,
        out_shape=pltpu.VMEM((count, width), F32),
        compiler_params=pltpu.CompilerParams(vmem_limit_bytes=8 * 2**20),
        cost_estimate=pl.CostEstimate(
            flops=4 * count * rows * width, bytes_accessed=8 * count * width, transcendentals=0
        ),
        name="advance",
    )(*fd_parts, par)


def boundary_kernel(order, half, pick, *refs):
    pieces = refs[: len(order)]
    out_ref, hi, lo = refs[len(order) :]
    my_case = lax.axis_index("case")
    for mask, piece in zip(order, pieces):
        size = piece.shape[0]
        slot = lax.rem(my_case ^ mask, half)
        span = pl.ds(pl.multiple_of(slot * size, size), size)
        hi[span, :], lo[span, :] = split_hi_lo(piece[...])
    out_ref[...] = two_pass(hi[...], lo[...], pick[...])


def boundary_columns(order, pick, pieces, flops):
    cols, width = pick.shape
    total = sum(piece.shape[0] for piece in pieces)
    vmem = pl.BlockSpec(memory_space=pltpu.VMEM)
    return pl.pallas_call(
        functools.partial(boundary_kernel, order, len(order)),
        in_specs=[vmem] * (1 + len(pieces)),
        out_specs=vmem,
        out_shape=pltpu.VMEM((total, width), F32),
        scratch_shapes=[pltpu.VMEM((total, cols), BF16)] * 2,
        compiler_params=pltpu.CompilerParams(vmem_limit_bytes=8 * 2**20),
        cost_estimate=pl.CostEstimate(flops=flops, bytes_accessed=1, transcendentals=0),
        name="boundary_columns",
    )(pick, *pieces)


def relay_of_square(square, power, rate):
    return jnp.maximum(jnp.exp2(power * jnp.log2(square + 1e-4)) - 1.0, 0.0) * rate


def case_kernel(tie_ref, fault_ref, out_ref):
    out_ref[0:1, :] = tie_ref[...]
    out_ref[1:2, :] = fault_ref[...]


def case_rows(tie_x, fault_z):
    vmem = pl.BlockSpec(memory_space=pltpu.VMEM)
    return pl.pallas_call(
        case_kernel,
        in_specs=[vmem, vmem],
        out_specs=vmem,
        out_shape=pltpu.VMEM((2, tie_x.shape[1]), F32),
        compiler_params=pltpu.CompilerParams(vmem_limit_bytes=2**20),
        cost_estimate=pl.CostEstimate(flops=2**34, bytes_accessed=2**20, transcendentals=0),
        name="case_rows",
    )(tie_x, fault_z)


def branch_kernel(half, n_ahead, g_ref, far_ref, case_ref, par_ref, fd_ref, near_ref, far_edge_ref, *refs):
    ahead = refs[:n_ahead]
    volt_hbm, relay_hbm, square_ref, worst_ref, vbuf, rbuf, uh, ul, vsem, rsem = refs[n_ahead:]
    rows, cases = vbuf.shape
    branches = par_ref.shape[0]
    late = square_ref.shape[0]
    ext = uh.shape[0]
    g = g_ref[...] + far_ref[...]
    g1, g2, g3 = g[0:1], g[1:2], g[2:3]
    ratio = g2 / (case_ref[0:1, :] + g1)
    amps = 1.0 / (g3 - g2 * ratio + case_ref[1:2, :])

    def sag_of(fd):
        return (fd[:, :cases] - fd[:, cases:] * ratio) * amps

    side = lax.axis_index("case") // half
    for edge_ref, place in ((near_ref, side), (far_edge_ref, 1 - side)):
        size = edge_ref.shape[0]
        edge = pl.ds(pl.multiple_of(rows + place * size, size), size)
        uh[edge, :], ul[edge, :] = split_hi_lo(sag_of(edge_ref[...]))
    tiles = rows // TILE
    rim = rim_tile(half, tiles)
    for t in range(tiles):
        span = tile_span(rim + t, tiles)
        sag = sag_of(fd_ref[pl.ds(t * TILE, TILE), :])
        vbuf[span, :] = 1.0 - sag
        uh[span, :], ul[span, :] = split_hi_lo(sag)
    copies = [pltpu.make_async_copy(vbuf, volt_hbm, vsem)]
    copies[0].start()

    def drops(par, first):
        count = par.shape[0]
        bus = lax.broadcasted_iota(jnp.int32, (count, ext - first), 1) + first
        ends = incidence(bus.astype(F32), par)
        span = pl.ds(first, ext - first)
        return jnp.dot(ends, uh[span, :], preferred_element_type=F32) + jnp.dot(
            ends, ul[span, :], preferred_element_type=F32
        )

    def square_of(drop, par, start):
        scaled = drop * par[:, 2:3]
        square = scaled * scaled
        largest = square[:, :128]
        for c in range(128, cases, 128):
            largest = jnp.maximum(largest, square[:, c : c + 128])
        for h in range(par.shape[0] // 128):
            worst_ref[pl.ds(start // 128 + h, 1), :] = jnp.max(
                largest[h * 128 : (h + 1) * 128, :].T, axis=0, keepdims=True
            )
        return square

    starts = [sum(part.shape[0] for part in ahead[:i]) for i in range(n_ahead + 1)]
    tiles = (branches - starts[-1]) // TILE
    for t in range(tiles):
        start = branches - (t + 1) * TILE
        par = par_ref[pl.ds(start, TILE), :]
        square = square_of(drops(par, 0), par, start)
        if start >= late:
            span = pl.ds(start - late, TILE)
            rbuf[span, :] = relay_of_square(square, par[:, 3:4], par[:, 4:5])
            target = relay_hbm.at[pl.ds(start, TILE)]
            copies.append(pltpu.make_async_copy(rbuf.at[span], target, rsem.at[t]))
        else:
            square_ref[pl.ds(start, TILE), :] = square
        for i in range(t, n_ahead if t == tiles - 1 else min(t + 1, n_ahead)):
            start, count = starts[i], ahead[i].shape[0]
            par = par_ref[pl.ds(start, count), :]
            drop = sag_of(ahead[i][...]) + drops(par, rows)
            square_ref[pl.ds(start, count), :] = square_of(drop, par, start)
        if len(copies) == t + 2:
            copies[-1].start()
    for copy in copies:
        copy.wait()


def screen_branches(g, g_far, case_par, par, fd, edges, ahead, n_case):
    count = case_par.shape[1]
    rows = fd.shape[0]
    branches = par.shape[0]
    late = sum(part.shape[0] for part in ahead) + TILE
    ext = rows + sum(edge.shape[0] for edge in edges)
    vmem = pl.BlockSpec(memory_space=pltpu.VMEM)
    hbm = pl.BlockSpec(memory_space=pltpu.HBM)
    return pl.pallas_call(
        functools.partial(branch_kernel, n_case // 2, len(ahead)),
        in_specs=[vmem] * (7 + len(ahead)),
        out_specs=[hbm, hbm, vmem, vmem],
        out_shape=[
            jax.ShapeDtypeStruct((rows, count), F32),
            jax.ShapeDtypeStruct((branches, count), F32),
            pltpu.VMEM((late, count), F32),
            pltpu.VMEM((branches // 128, 128), F32),
        ],
        scratch_shapes=[
            pltpu.VMEM((rows, count), F32),
            pltpu.VMEM((branches - late, count), F32),
            pltpu.VMEM((ext, count), BF16),
            pltpu.VMEM((ext, count), BF16),
            pltpu.SemaphoreType.DMA,
            pltpu.SemaphoreType.DMA((branches // TILE,)),
        ],
        compiler_params=pltpu.CompilerParams(vmem_limit_bytes=24 * 2**20),
        name="screen_branches",
    )(g, g_far, case_par, par, fd, *edges, *ahead)


def late_kernel(square_ref, par_ref, relay_in, relay_hbm, rbuf, sems):
    copies = []
    for t in range(square_ref.shape[0] // TILE):
        span = pl.ds(t * TILE, TILE)
        par = par_ref[span, :]
        rbuf[span, :] = relay_of_square(square_ref[span, :], par[:, 3:4], par[:, 4:5])
        copies.append(pltpu.make_async_copy(rbuf.at[span], relay_hbm.at[span], sems.at[t]))
        copies[-1].start()
    for copy in copies:
        copy.wait()


def late_relays(square, par, relay_rate):
    vmem = pl.BlockSpec(memory_space=pltpu.VMEM)
    hbm = pl.BlockSpec(memory_space=pltpu.HBM)
    return pl.pallas_call(
        late_kernel,
        in_specs=[vmem, vmem, hbm],
        out_specs=hbm,
        out_shape=jax.ShapeDtypeStruct(relay_rate.shape, F32),
        input_output_aliases={2: 0},
        scratch_shapes=[
            pltpu.VMEM(square.shape, F32),
            pltpu.SemaphoreType.DMA((square.shape[0] // TILE,)),
        ],
        compiler_params=pltpu.CompilerParams(vmem_limit_bytes=8 * 2**20),
        cost_estimate=pl.CostEstimate(
            flops=8 * square.size, bytes_accessed=8 * square.size, transcendentals=2 * square.size
        ),
        name="late_relays",
    )(square, par, relay_rate)


def per_device(
    z_columns,
    resident_bus,
    fault_col,
    switch_cols,
    tie_x,
    fault_z,
    boundary_send,
    branch_ends,
    branch_x,
    pickup,
    tds,
    curve,
):
    n_bus, n_case = lax.axis_size("bus"), lax.axis_size("case")
    half = n_case // 2
    fault, switch = fault_col[None], switch_cols.T
    send, z, pick = stage(z_columns, boundary_send, fault, switch, n_case)
    pairs = []
    for s in range(n_bus):
        for c in range(n_case):
            to = s + 1 if c < half else s - 1
            if 0 <= to < n_bus:
                pairs.append((s * n_case + c, to * n_case + c))
    own = lax.ppermute(send, ("bus", "case"), pairs)

    by_lines = [x.reshape(-1, 128) for x in (branch_x, pickup, tds, curve)]
    fd, g, par, *fd_parts = pick_columns(
        z,
        pick,
        fault,
        switch,
        resident_bus[None],
        z_columns,
        branch_ends.T,
        by_lines[:3],
        by_lines[3],
        n_case,
    )

    def swap_over_bus(g, bit):
        return lax.ppermute(g, "bus", [(i, i ^ bit) for i in range(n_bus)])

    def after(first, *values):
        return lax.optimization_barrier((first, *values))[1:]

    (own,) = after(g, own)
    other = lax.ppermute(own, "case", [(i, i ^ half) for i in range(n_case)])
    ahead = []
    sizes = [par.shape[0] // 4, par.shape[0] // 4]
    bit = 1
    while bit < n_bus // 2:
        far = swap_over_bus(g, bit)
        if bit == 2:
            (own,) = after(g, own)
        if len(ahead) < len(sizes):
            i = len(ahead)
            ahead.append(advance(fd_parts, par, sum(sizes[:i]), sizes[i], n_case))
            (far,) = after(ahead[-1], far)
        g = g + far
        bit *= 2
    g_far = swap_over_bus(g, n_bus // 2)
    (other,) = after(g, other)
    edges = []
    for piece, flops in ((own, 2**29), (other, 1)):
        pieces, order = [piece], [0]
        bit = half // 2
        while bit:
            swap = [(i, i ^ bit) for i in range(n_case)]
            pieces = pieces + [lax.ppermute(x, "case", swap) for x in pieces]
            order = order + [m ^ bit for m in order]
            bit //= 2
        edges.append(boundary_columns(order, pick, pieces, flops))
    voltage, relay_rate, square, worst = screen_branches(
        g, g_far, case_rows(tie_x[None], fault_z[None]), par, fd, edges, ahead, n_case
    )
    others = [
        lax.ppermute(worst, "case", [(i, i ^ m) for i in range(n_case)])
        for m in range(n_case - 1, 0, -1)
    ]
    relay_rate = late_relays(square, par, relay_rate)
    half_power, factor = curve_constants(curve)
    worst = functools.reduce(jnp.maximum, others, worst).reshape(-1)
    worst_rate = relay_of_square(worst, half_power, 1.0 / (factor * tds))
    return (voltage, relay_rate, worst_rate)


def solution(mesh):
    in_specs = (
        P("bus", None),
        P(),
        P("case"),
        P("case", None),
        P("case"),
        P("case"),
        P(),
        P("bus", None),
        P("bus"),
        P("bus"),
        P("bus"),
        P("bus"),
    )
    out_specs = (P("bus", "case"), P("bus", "case"), P("bus"))
    return jax.shard_map(
        per_device, mesh=mesh, in_specs=in_specs, out_specs=out_specs, check_vma=False
    )
```

```python
import functools

import jax
import jax.numpy as jnp
from jax import lax
from jax.experimental import pallas as pl
from jax.experimental.pallas import tpu as pltpu
from jax.sharding import PartitionSpec as P

TILE = 256
STAGED = 2
F32 = jnp.float32
BF16 = jnp.bfloat16


def split_hi_lo(value):
    hi = value.astype(BF16)
    return hi, (value - hi.astype(F32)).astype(BF16)


def two_pass(hi, lo, rhs):
    return jnp.dot(hi, rhs, preferred_element_type=F32) + jnp.dot(
        lo, rhs, preferred_element_type=F32
    )


def in_hbm(*arrays):
    return [pltpu.with_memory_space_constraint(x, pltpu.HBM) for x in arrays]


def rim_tile(half, tiles):
    return (1 - lax.axis_index("case") // half) * (tiles - 1)


def tile_span(t, tiles):
    return pl.ds(pl.multiple_of(lax.rem(t, tiles) * TILE, TILE), TILE)


def stage_kernel(
    half, z_hbm, lists_hbm, fault_hbm, switch_hbm, send_ref, z_ref, pick_ref, lists, cases, sems
):
    tiles = z_hbm.shape[0] // TILE
    piece = send_ref.shape[0]
    my_bus, my_case = lax.axis_index("bus"), lax.axis_index("case")
    rim = rim_tile(half, tiles)
    loads = [
        pltpu.make_async_copy(fault_hbm, cases.at[pl.ds(0, 1)], sems.at[0]),
        pltpu.make_async_copy(switch_hbm, cases.at[pl.ds(8, 2)], sems.at[1]),
        pltpu.make_async_copy(lists_hbm.at[my_bus], lists, sems.at[2]),
    ]
    for t in range(z_ref.shape[0] // TILE):
        target = z_ref.at[pl.ds(t * TILE, TILE)]
        source = z_hbm.at[tile_span(rim + t, tiles)]
        loads.append(pltpu.make_async_copy(source, target, sems.at[3 + t]))
    for load in loads:
        load.start()
    for load in loads[:2]:
        load.wait()
    fill_picks(cases[0:1, :], cases[8:10, :], pick_ref)
    for load in loads[2:4]:
        load.wait()
    down = my_case // half
    base = (my_case % half) * piece
    first = rim * TILE
    for i in range(piece):
        send_ref[pl.ds(i, 1), :] = z_ref[pl.ds(lists[1 - down, base + i] - first, 1), :]
    for load in loads[4:]:
        load.wait()


def stage(z_columns, boundary_send, fault, switch, n_case):
    cols = z_columns.shape[1]
    half = n_case // 2
    count = fault.shape[1]
    return pl.pallas_call(
        functools.partial(stage_kernel, half),
        in_specs=[pl.BlockSpec(memory_space=pltpu.HBM)] * 4,
        out_specs=[pl.BlockSpec(memory_space=pltpu.VMEM)] * 3,
        out_shape=[
            pltpu.VMEM((boundary_send.shape[2] // half, cols), F32),
            pltpu.VMEM((STAGED * TILE, cols), F32),
            pltpu.VMEM((cols, 2 * count), BF16),
        ],
        scratch_shapes=[
            pltpu.SMEM(boundary_send.shape[1:], jnp.int32),
            pltpu.VMEM((16, count), jnp.int32),
            pltpu.SemaphoreType.DMA((STAGED + 3,)),
        ],
        compiler_params=pltpu.CompilerParams(vmem_limit_bytes=4 * 2**20),
        name="stage",
    )(*in_hbm(z_columns, boundary_send, fault, switch))


def fill_picks(f, ab, pick):
    cols, count = pick.shape[0], f.shape[1]
    a, b = ab[0:1, :], ab[1:2, :]
    for t in range(cols // TILE):
        k = lax.broadcasted_iota(jnp.int32, (TILE, count), 0) + t * TILE
        span = pl.ds(t * TILE, TILE)
        pick[span, :count] = jnp.where(k == f, 1.0, 0.0).astype(BF16)
        pick[span, count:] = jnp.where(k == a, 1.0, jnp.where(k == b, -1.0, 0.0)).astype(BF16)


def columns_kernel(
    half,
    z_ref,
    pick,
    fault_ref,
    switch_ref,
    resident_ref,
    z_hbm,
    ends_hbm,
    x_hbm,
    pickup_hbm,
    tds_hbm,
    curve_hbm,
    fd_ref,
    g_ref,
    par_ref,
    fd_hi,
    fd_lo,
    later,
    ends,
    floats,
    curves,
    sems,
):
    rows, cols = z_hbm.shape
    cases = fault_ref.shape[1]
    tiles = rows // TILE
    rim = rim_tile(half, tiles)
    loads = []
    for t in range(STAGED, tiles):
        target = later.at[pl.ds((t - STAGED) * TILE, TILE)]
        source = z_hbm.at[tile_span(rim + t, tiles)]
        loads.append(pltpu.make_async_copy(source, target, sems.at[t]))
    small = [
        pltpu.make_async_copy(source, target, sems.at[tiles + i])
        for i, (source, target) in enumerate(
            [
                (ends_hbm, ends),
                (x_hbm, floats.at[0]),
                (pickup_hbm, floats.at[1]),
                (tds_hbm, floats.at[2]),
                (curve_hbm, curves),
            ]
        )
    ]
    for load in loads + small:
        load.start()
    f, a, b = fault_ref[...], switch_ref[0:1, :], switch_ref[1:2, :]
    resident = resident_ref[...] - lax.axis_index("bus") * rows
    g1 = jnp.zeros((1, cases), F32)
    g2 = jnp.zeros((1, cases), F32)
    g3 = jnp.zeros((1, cases), F32)
    k = lax.broadcasted_iota(jnp.int32, (TILE, cols), 1)
    for t in range(tiles + 1):
        if t == STAGED:
            for load in loads + small:
                load.wait()
        if t < tiles:
            if t < STAGED:
                z = z_ref[pl.ds(t * TILE, TILE), :]
            else:
                z = later[pl.ds((t - STAGED) * TILE, TILE), :]
            hi, lo = split_hi_lo(z)
            fd_ref[pl.ds(t * TILE, TILE), :] = two_pass(hi, lo, pick[...])
        if t == STAGED:
            gain = 1.0 / (floats[0] * floats[1])
            half_power, factor = curve_constants(curves[...])
            rate = 1.0 / (factor * floats[2])
            for c in range(gain.shape[0]):
                line = pl.ds(c * 128, 128)
                lines = [ends[:, line].astype(F32)]
                lines += [x[c : c + 1] for x in (gain, half_power, rate)]
                par_ref[line, :] = jnp.concatenate(lines + [jnp.zeros((3, 128), F32)]).T
        if t > 0:
            span = pl.ds((t - 1) * TILE, TILE)
            first = tile_span(rim + t - 1, tiles).start
            row = lax.broadcasted_iota(jnp.int32, (TILE, cols), 0) + first
            owner = jnp.max(jnp.where(row == resident, k, -1), axis=1, keepdims=True)
            fd_hi[span, :], fd_lo[span, :] = split_hi_lo(fd_ref[span, :])
            fault, diff = fd_ref[span, :cases], fd_ref[span, cases:]
            at_f = owner == f
            g3 += jnp.sum(jnp.where(at_f, fault, 0.0), axis=0, keepdims=True)
            g2 += jnp.sum(jnp.where(at_f, diff, 0.0), axis=0, keepdims=True)
            g1 += jnp.sum(
                jnp.where(owner == a, diff, jnp.where(owner == b, -diff, 0.0)),
                axis=0,
                keepdims=True,
            )
    g_ref[...] = jnp.concatenate([g1, g2, g3, jnp.zeros((g_ref.shape[0] - 3, cases), F32)])


def pick_columns(z, pick, fault, switch, resident, z_columns, ends, values, curve, n_case):
    rows, cols = z_columns.shape
    count = fault.shape[1]
    lines = curve.shape[0]
    vmem = pl.BlockSpec(memory_space=pltpu.VMEM)
    return pl.pallas_call(
        functools.partial(columns_kernel, n_case // 2),
        in_specs=[vmem] * 5 + [pl.BlockSpec(memory_space=pltpu.HBM)] * 6,
        out_specs=[vmem] * 5,
        out_shape=[
            pltpu.VMEM((rows, 2 * count), F32),
            pltpu.VMEM((4, count), F32),
            pltpu.VMEM((lines * 128, 8), F32),
            pltpu.VMEM((rows, 2 * count), BF16),
            pltpu.VMEM((rows, 2 * count), BF16),
        ],
        scratch_shapes=[
            pltpu.VMEM((rows - STAGED * TILE, cols), F32),
            pltpu.VMEM(ends.shape, jnp.int32),
            pltpu.VMEM((3, lines, 128), F32),
            pltpu.VMEM((lines, 128), jnp.int32),
            pltpu.SemaphoreType.DMA((rows // TILE + 5,)),
        ],
        compiler_params=pltpu.CompilerParams(vmem_limit_bytes=20 * 2**20),
        name="pick_columns",
    )(z, pick, fault, switch, resident, *in_hbm(z_columns, ends, *values, curve))


def curve_constants(curve):
    half_power = jnp.where(curve == 0, 0.01, jnp.where(curve == 1, 0.5, 1.0)).astype(F32)
    factor = jnp.where(curve == 0, 0.14, jnp.where(curve == 1, 13.5, 80.0)).astype(F32)
    return half_power, factor


def incidence(bus, par):
    return jnp.where(bus == par[:, 1:2], 1.0, jnp.where(bus == par[:, 0:1], -1.0, 0.0)).astype(BF16)


def advance_kernel(half, start, fd_hi, fd_lo, par_ref, out_ref):
    rows = fd_hi.shape[0]
    count = out_ref.shape[0]
    bus = lax.broadcasted_iota(jnp.int32, (count, rows), 1)
    bus = bus + rim_tile(half, rows // TILE) * TILE
    bus = jnp.where(bus >= rows, bus - rows, bus).astype(F32)
    ends = incidence(bus, par_ref[pl.ds(start, count), :])
    out_ref[...] = jnp.dot(ends, fd_hi[...], preferred_element_type=F32) + jnp.dot(
        ends, fd_lo[...], preferred_element_type=F32
    )


def advance(fd_parts, par, start, count, n_case):
    rows, width = fd_parts[0].shape
    vmem = pl.BlockSpec(memory_space=pltpu.VMEM)
    return pl.pallas_call(
        functools.partial(advance_kernel, n_case // 2, start),
        in_specs=[vmem] * 3,
        out_specs=vmem,
        out_shape=pltpu.VMEM((count, width), F32),
        compiler_params=pltpu.CompilerParams(vmem_limit_bytes=8 * 2**20),
        cost_estimate=pl.CostEstimate(
            flops=4 * count * rows * width, bytes_accessed=8 * count * width, transcendentals=0
        ),
        name="advance",
    )(*fd_parts, par)


def boundary_kernel(order, half, pick, *refs):
    pieces = refs[: len(order)]
    out_ref, hi, lo = refs[len(order) :]
    my_case = lax.axis_index("case")
    for mask, piece in zip(order, pieces):
        size = piece.shape[0]
        slot = lax.rem(my_case ^ mask, half)
        span = pl.ds(pl.multiple_of(slot * size, size), size)
        hi[span, :], lo[span, :] = split_hi_lo(piece[...])
    out_ref[...] = two_pass(hi[...], lo[...], pick[...])


def boundary_columns(order, pick, pieces, flops):
    cols, width = pick.shape
    total = sum(piece.shape[0] for piece in pieces)
    vmem = pl.BlockSpec(memory_space=pltpu.VMEM)
    return pl.pallas_call(
        functools.partial(boundary_kernel, order, len(order)),
        in_specs=[vmem] * (1 + len(pieces)),
        out_specs=vmem,
        out_shape=pltpu.VMEM((total, width), F32),
        scratch_shapes=[pltpu.VMEM((total, cols), BF16)] * 2,
        compiler_params=pltpu.CompilerParams(vmem_limit_bytes=8 * 2**20),
        cost_estimate=pl.CostEstimate(flops=flops, bytes_accessed=1, transcendentals=0),
        name="boundary_columns",
    )(pick, *pieces)


def relay_of_square(square, power, rate):
    return jnp.maximum(jnp.exp2(power * jnp.log2(square + 1e-4)) - 1.0, 0.0) * rate


def case_kernel(tie_ref, fault_ref, out_ref):
    out_ref[0:1, :] = tie_ref[...]
    out_ref[1:2, :] = fault_ref[...]


def case_rows(tie_x, fault_z):
    vmem = pl.BlockSpec(memory_space=pltpu.VMEM)
    return pl.pallas_call(
        case_kernel,
        in_specs=[vmem, vmem],
        out_specs=vmem,
        out_shape=pltpu.VMEM((2, tie_x.shape[1]), F32),
        compiler_params=pltpu.CompilerParams(vmem_limit_bytes=2**20),
        cost_estimate=pl.CostEstimate(flops=2**34, bytes_accessed=2**20, transcendentals=0),
        name="case_rows",
    )(tie_x, fault_z)


def branch_kernel(half, n_ahead, g_ref, far_ref, case_ref, par_ref, fd_ref, near_ref, far_edge_ref, *refs):
    ahead = refs[:n_ahead]
    volt_hbm, square_ref, worst_ref, vbuf, uh, ul, vsem = refs[n_ahead:]
    rows, cases = vbuf.shape
    branches = par_ref.shape[0]
    ext = uh.shape[0]
    g = g_ref[...] + far_ref[...]
    g1, g2, g3 = g[0:1], g[1:2], g[2:3]
    ratio = g2 / (case_ref[0:1, :] + g1)
    amps = 1.0 / (g3 - g2 * ratio + case_ref[1:2, :])

    def sag_of(fd):
        return (fd[:, :cases] - fd[:, cases:] * ratio) * amps

    side = lax.axis_index("case") // half
    for edge_ref, place in ((near_ref, side), (far_edge_ref, 1 - side)):
        size = edge_ref.shape[0]
        edge = pl.ds(pl.multiple_of(rows + place * size, size), size)
        uh[edge, :], ul[edge, :] = split_hi_lo(sag_of(edge_ref[...]))
    tiles = rows // TILE
    rim = rim_tile(half, tiles)
    for t in range(tiles):
        span = tile_span(rim + t, tiles)
        sag = sag_of(fd_ref[pl.ds(t * TILE, TILE), :])
        vbuf[span, :] = 1.0 - sag
        uh[span, :], ul[span, :] = split_hi_lo(sag)
    copy = pltpu.make_async_copy(vbuf, volt_hbm, vsem)
    copy.start()

    def drops(par, first):
        count = par.shape[0]
        bus = lax.broadcasted_iota(jnp.int32, (count, ext - first), 1) + first
        ends = incidence(bus.astype(F32), par)
        span = pl.ds(first, ext - first)
        return jnp.dot(ends, uh[span, :], preferred_element_type=F32) + jnp.dot(
            ends, ul[span, :], preferred_element_type=F32
        )

    def square_of(drop, par, start):
        scaled = drop * par[:, 2:3]
        square = scaled * scaled
        largest = square[:, :128]
        for c in range(128, cases, 128):
            largest = jnp.maximum(largest, square[:, c : c + 128])
        for h in range(par.shape[0] // 128):
            worst_ref[pl.ds(start // 128 + h, 1), :] = jnp.max(
                largest[h * 128 : (h + 1) * 128, :].T, axis=0, keepdims=True
            )
        return square

    def finish(drop, par, start):
        square_ref[pl.ds(start, par.shape[0]), :] = square_of(drop, par, start)

    starts = [sum(part.shape[0] for part in ahead[:i]) for i in range(n_ahead + 1)]
    whole = list(range(starts.pop(), branches, TILE))
    for n in range(max(len(whole), n_ahead)):
        if n < len(whole):
            par = par_ref[pl.ds(whole[n], TILE), :]
            finish(drops(par, 0), par, whole[n])
        if n < n_ahead:
            par = par_ref[pl.ds(starts[n], ahead[n].shape[0]), :]
            finish(sag_of(ahead[n][...]) + drops(par, rows), par, starts[n])
    copy.wait()


def screen_branches(g, g_far, case_par, par, fd, edges, ahead, n_case):
    count = case_par.shape[1]
    rows = fd.shape[0]
    branches = par.shape[0]
    ext = rows + sum(edge.shape[0] for edge in edges)
    vmem = pl.BlockSpec(memory_space=pltpu.VMEM)
    hbm = pl.BlockSpec(memory_space=pltpu.HBM)
    return pl.pallas_call(
        functools.partial(branch_kernel, n_case // 2, len(ahead)),
        in_specs=[vmem] * (7 + len(ahead)),
        out_specs=[hbm, vmem, vmem],
        out_shape=[
            jax.ShapeDtypeStruct((rows, count), F32),
            pltpu.VMEM((branches, count), F32),
            pltpu.VMEM((branches // 128, 128), F32),
        ],
        scratch_shapes=[
            pltpu.VMEM((rows, count), F32),
            pltpu.VMEM((ext, count), BF16),
            pltpu.VMEM((ext, count), BF16),
            pltpu.SemaphoreType.DMA,
        ],
        compiler_params=pltpu.CompilerParams(vmem_limit_bytes=24 * 2**20),
        name="screen_branches",
    )(g, g_far, case_par, par, fd, *edges, *ahead)


def relay_kernel(square_ref, par_ref, relay_hbm, rbuf, sems):
    rows = square_ref.shape[0]
    copies = []
    first = 0
    while first < rows:
        count = TILE if first + 2 * TILE <= rows else TILE // 2
        span = pl.ds(first, count)
        par = par_ref[span, :]
        rbuf[span, :] = relay_of_square(square_ref[span, :], par[:, 3:4], par[:, 4:5])
        sem = sems.at[len(copies)]
        copies.append(pltpu.make_async_copy(rbuf.at[span], relay_hbm.at[span], sem))
        copies[-1].start()
        first += count
    for copy in copies:
        copy.wait()


def relay_rates(square, par):
    rows = square.shape[0]
    vmem = pl.BlockSpec(memory_space=pltpu.VMEM)
    return pl.pallas_call(
        relay_kernel,
        in_specs=[vmem, vmem],
        out_specs=pl.BlockSpec(memory_space=pltpu.HBM),
        out_shape=jax.ShapeDtypeStruct(square.shape, F32),
        scratch_shapes=[
            pltpu.VMEM(square.shape, F32),
            pltpu.SemaphoreType.DMA((rows // TILE + 1,)),
        ],
        compiler_params=pltpu.CompilerParams(vmem_limit_bytes=8 * 2**20),
        cost_estimate=pl.CostEstimate(
            flops=8 * square.size, bytes_accessed=8 * square.size, transcendentals=2 * square.size
        ),
        name="relay_rates",
    )(square, par)


def per_device(
    z_columns,
    resident_bus,
    fault_col,
    switch_cols,
    tie_x,
    fault_z,
    boundary_send,
    branch_ends,
    branch_x,
    pickup,
    tds,
    curve,
):
    n_bus, n_case = lax.axis_size("bus"), lax.axis_size("case")
    half = n_case // 2
    fault, switch = fault_col[None], switch_cols.T
    send, z, pick = stage(z_columns, boundary_send, fault, switch, n_case)
    pairs = []
    for s in range(n_bus):
        for c in range(n_case):
            to = s + 1 if c < half else s - 1
            if 0 <= to < n_bus:
                pairs.append((s * n_case + c, to * n_case + c))
    own = lax.ppermute(send, ("bus", "case"), pairs)

    by_lines = [x.reshape(-1, 128) for x in (branch_x, pickup, tds, curve)]
    fd, g, par, *fd_parts = pick_columns(
        z,
        pick,
        fault,
        switch,
        resident_bus[None],
        z_columns,
        branch_ends.T,
        by_lines[:3],
        by_lines[3],
        n_case,
    )

    def swap_over_bus(g, bit):
        return lax.ppermute(g, "bus", [(i, i ^ bit) for i in range(n_bus)])

    def after(first, *values):
        return lax.optimization_barrier((first, *values))[1:]

    (own,) = after(g, own)
    other = lax.ppermute(own, "case", [(i, i ^ half) for i in range(n_case)])
    ahead = []
    sizes = [par.shape[0] // 12 * i for i in (3, 5)]
    bits = [2**i for i in range(1, (n_bus - 1).bit_length())]
    bits.insert(len(bits) - 1, 1)
    for n, bit in enumerate(bits[:-1]):
        far = swap_over_bus(g, bit)
        if n == 1:
            (own,) = after(g, own)
        if n < len(sizes):
            ahead.append(advance(fd_parts, par, sum(sizes[:n]), sizes[n], n_case))
            (far,) = after(ahead[n], far)
        g = g + far
    g_far = swap_over_bus(g, bits[-1])
    (other,) = after(g, other)
    edges = []
    for piece, flops in ((own, 2**29), (other, 1)):
        pieces, order = [piece], [0]
        bit = half // 2
        while bit:
            swap = [(i, i ^ bit) for i in range(n_case)]
            pieces = pieces + [lax.ppermute(x, "case", swap) for x in pieces]
            order = order + [m ^ bit for m in order]
            bit //= 2
        edges.append(boundary_columns(order, pick, pieces, flops))
    voltage, square, worst = screen_branches(
        g, g_far, case_rows(tie_x[None], fault_z[None]), par, fd, edges, ahead, n_case
    )
    others = [
        lax.ppermute(worst, "case", [(i, i ^ m) for i in range(n_case)])
        for m in range(n_case - 1, 0, -1)
    ]
    relay_rate = relay_rates(square, par)
    half_power, factor = curve_constants(curve)
    worst = functools.reduce(jnp.maximum, others, worst).reshape(-1)
    worst_rate = relay_of_square(worst, half_power, 1.0 / (factor * tds))
    return (voltage, relay_rate, worst_rate)


def solution(mesh):
    in_specs = (
        P("bus", None),
        P(),
        P("case"),
        P("case", None),
        P("case"),
        P("case"),
        P(),
        P("bus", None),
        P("bus"),
        P("bus"),
        P("bus"),
        P("bus"),
    )
    out_specs = (P("bus", "case"), P("bus", "case"), P("bus"))
    return jax.shard_map(
        per_device, mesh=mesh, in_specs=in_specs, out_specs=out_specs, check_vma=False
    )
```

```python
import functools

import jax
import jax.numpy as jnp
from jax import lax
from jax.experimental import pallas as pl
from jax.experimental.pallas import tpu as pltpu
from jax.sharding import PartitionSpec as P

TILE = 256
STAGED = 2
F32 = jnp.float32
BF16 = jnp.bfloat16


def split_hi_lo(value):
    hi = value.astype(BF16)
    return hi, (value - hi.astype(F32)).astype(BF16)


def two_pass(hi, lo, rhs):
    return jnp.dot(hi, rhs, preferred_element_type=F32) + jnp.dot(
        lo, rhs, preferred_element_type=F32
    )


def in_hbm(*arrays):
    return [pltpu.with_memory_space_constraint(x, pltpu.HBM) for x in arrays]


def rim_tile(half, tiles):
    return (1 - lax.axis_index("case") // half) * (tiles - 1)


def tile_span(t, tiles):
    return pl.ds(pl.multiple_of(lax.rem(t, tiles) * TILE, TILE), TILE)


def stage_kernel(
    half, z_hbm, lists_hbm, fault_hbm, switch_hbm, send_ref, z_ref, pick_ref, lists, cases, sems
):
    tiles = z_hbm.shape[0] // TILE
    piece = send_ref.shape[0]
    my_bus, my_case = lax.axis_index("bus"), lax.axis_index("case")
    rim = rim_tile(half, tiles)
    loads = [
        pltpu.make_async_copy(fault_hbm, cases.at[pl.ds(0, 1)], sems.at[0]),
        pltpu.make_async_copy(switch_hbm, cases.at[pl.ds(8, 2)], sems.at[1]),
        pltpu.make_async_copy(lists_hbm.at[my_bus], lists, sems.at[2]),
    ]
    for t in range(z_ref.shape[0] // TILE):
        target = z_ref.at[pl.ds(t * TILE, TILE)]
        source = z_hbm.at[tile_span(rim + t, tiles)]
        loads.append(pltpu.make_async_copy(source, target, sems.at[3 + t]))
    for load in loads:
        load.start()
    for load in loads[:2]:
        load.wait()
    fill_picks(cases[0:1, :], cases[8:10, :], pick_ref)
    for load in loads[2:4]:
        load.wait()
    down = my_case // half
    base = (my_case % half) * piece
    first = rim * TILE
    for i in range(piece):
        row = jnp.clip(lists[1 - down, base + i] - first, 0, TILE - 1)
        send_ref[pl.ds(i, 1), :] = z_ref[pl.ds(row, 1), :]
    for load in loads[4:]:
        load.wait()


def stage(z_columns, boundary_send, fault, switch, n_case):
    cols = z_columns.shape[1]
    half = n_case // 2
    count = fault.shape[1]
    return pl.pallas_call(
        functools.partial(stage_kernel, half),
        in_specs=[pl.BlockSpec(memory_space=pltpu.HBM)] * 4,
        out_specs=[pl.BlockSpec(memory_space=pltpu.VMEM)] * 3,
        out_shape=[
            pltpu.VMEM((boundary_send.shape[2] // half, cols), F32),
            pltpu.VMEM((STAGED * TILE, cols), F32),
            pltpu.VMEM((cols, 2 * count), BF16),
        ],
        scratch_shapes=[
            pltpu.SMEM(boundary_send.shape[1:], jnp.int32),
            pltpu.VMEM((16, count), jnp.int32),
            pltpu.SemaphoreType.DMA((STAGED + 3,)),
        ],
        compiler_params=pltpu.CompilerParams(vmem_limit_bytes=4 * 2**20),
        name="stage",
    )(*in_hbm(z_columns, boundary_send, fault, switch))


def fill_picks(f, ab, pick):
    cols, count = pick.shape[0], f.shape[1]
    a, b = ab[0:1, :], ab[1:2, :]
    for t in range(cols // TILE):
        k = lax.broadcasted_iota(jnp.int32, (TILE, count), 0) + t * TILE
        span = pl.ds(t * TILE, TILE)
        pick[span, :count] = jnp.where(k == f, 1.0, 0.0).astype(BF16)
        pick[span, count:] = jnp.where(k == a, 1.0, jnp.where(k == b, -1.0, 0.0)).astype(BF16)


def columns_kernel(
    half,
    z_ref,
    pick,
    fault_ref,
    switch_ref,
    resident_ref,
    z_hbm,
    ends_hbm,
    x_hbm,
    pickup_hbm,
    tds_hbm,
    curve_hbm,
    fd_ref,
    g_ref,
    par_ref,
    fd_hi,
    fd_lo,
    later,
    ends,
    floats,
    curves,
    sems,
):
    rows, cols = z_hbm.shape
    cases = fault_ref.shape[1]
    tiles = rows // TILE
    rim = rim_tile(half, tiles)
    loads = []
    for t in range(STAGED, tiles):
        target = later.at[pl.ds((t - STAGED) * TILE, TILE)]
        source = z_hbm.at[tile_span(rim + t, tiles)]
        loads.append(pltpu.make_async_copy(source, target, sems.at[t]))
    small = [
        pltpu.make_async_copy(source, target, sems.at[tiles + i])
        for i, (source, target) in enumerate(
            [
                (ends_hbm, ends),
                (x_hbm, floats.at[0]),
                (pickup_hbm, floats.at[1]),
                (tds_hbm, floats.at[2]),
                (curve_hbm, curves),
            ]
        )
    ]
    for load in loads + small:
        load.start()
    f, a, b = fault_ref[...], switch_ref[0:1, :], switch_ref[1:2, :]
    resident = resident_ref[...] - lax.axis_index("bus") * rows
    g1 = jnp.zeros((1, cases), F32)
    g2 = jnp.zeros((1, cases), F32)
    g3 = jnp.zeros((1, cases), F32)
    k = lax.broadcasted_iota(jnp.int32, (TILE, cols), 1)
    for t in range(tiles + 1):
        if t == STAGED:
            for load in loads + small:
                load.wait()
        if t < tiles:
            if t < STAGED:
                z = z_ref[pl.ds(t * TILE, TILE), :]
            else:
                z = later[pl.ds((t - STAGED) * TILE, TILE), :]
            hi, lo = split_hi_lo(z)
            fd_ref[pl.ds(t * TILE, TILE), :] = two_pass(hi, lo, pick[...])
        if t == STAGED:
            gain = 1.0 / (floats[0] * floats[1])
            half_power, factor = curve_constants(curves[...])
            rate = 1.0 / (factor * floats[2])
            for c in range(gain.shape[0]):
                line = pl.ds(c * 128, 128)
                lines = [ends[:, line].astype(F32)]
                lines += [x[c : c + 1] for x in (gain, half_power, rate)]
                par_ref[line, :] = jnp.concatenate(lines + [jnp.zeros((3, 128), F32)]).T
        if t > 0:
            span = pl.ds((t - 1) * TILE, TILE)
            first = tile_span(rim + t - 1, tiles).start
            row = lax.broadcasted_iota(jnp.int32, (TILE, cols), 0) + first
            owner = jnp.max(jnp.where(row == resident, k, -1), axis=1, keepdims=True)
            fd_hi[span, :], fd_lo[span, :] = split_hi_lo(fd_ref[span, :])
            fault, diff = fd_ref[span, :cases], fd_ref[span, cases:]
            at_f = owner == f
            g3 += jnp.sum(jnp.where(at_f, fault, 0.0), axis=0, keepdims=True)
            g2 += jnp.sum(jnp.where(at_f, diff, 0.0), axis=0, keepdims=True)
            g1 += jnp.sum(
                jnp.where(owner == a, diff, jnp.where(owner == b, -diff, 0.0)),
                axis=0,
                keepdims=True,
            )
    g_ref[...] = jnp.concatenate([g1, g2, g3, jnp.zeros((g_ref.shape[0] - 3, cases), F32)])


def pick_columns(z, pick, fault, switch, resident, z_columns, ends, values, curve, n_case):
    rows, cols = z_columns.shape
    count = fault.shape[1]
    lines = curve.shape[0]
    vmem = pl.BlockSpec(memory_space=pltpu.VMEM)
    return pl.pallas_call(
        functools.partial(columns_kernel, n_case // 2),
        in_specs=[vmem] * 5 + [pl.BlockSpec(memory_space=pltpu.HBM)] * 6,
        out_specs=[vmem] * 5,
        out_shape=[
            pltpu.VMEM((rows, 2 * count), F32),
            pltpu.VMEM((4, count), F32),
            pltpu.VMEM((lines * 128, 8), F32),
            pltpu.VMEM((rows, 2 * count), BF16),
            pltpu.VMEM((rows, 2 * count), BF16),
        ],
        scratch_shapes=[
            pltpu.VMEM((rows - STAGED * TILE, cols), F32),
            pltpu.VMEM(ends.shape, jnp.int32),
            pltpu.VMEM((3, lines, 128), F32),
            pltpu.VMEM((lines, 128), jnp.int32),
            pltpu.SemaphoreType.DMA((rows // TILE + 5,)),
        ],
        compiler_params=pltpu.CompilerParams(vmem_limit_bytes=20 * 2**20),
        name="pick_columns",
    )(z, pick, fault, switch, resident, *in_hbm(z_columns, ends, *values, curve))


def curve_constants(curve):
    half_power = jnp.where(curve == 0, 0.01, jnp.where(curve == 1, 0.5, 1.0)).astype(F32)
    factor = jnp.where(curve == 0, 0.14, jnp.where(curve == 1, 13.5, 80.0)).astype(F32)
    return half_power, factor


def incidence(bus, par):
    return jnp.where(bus == par[:, 1:2], 1.0, jnp.where(bus == par[:, 0:1], -1.0, 0.0)).astype(BF16)


def advance_kernel(half, start, fd_hi, fd_lo, par_ref, out_ref):
    rows = fd_hi.shape[0]
    count = out_ref.shape[0]
    bus = lax.broadcasted_iota(jnp.int32, (count, rows), 1)
    bus = bus + rim_tile(half, rows // TILE) * TILE
    bus = jnp.where(bus >= rows, bus - rows, bus).astype(F32)
    ends = incidence(bus, par_ref[pl.ds(start, count), :])
    out_ref[...] = jnp.dot(ends, fd_hi[...], preferred_element_type=F32) + jnp.dot(
        ends, fd_lo[...], preferred_element_type=F32
    )


def advance(fd_parts, par, start, count, n_case):
    rows, width = fd_parts[0].shape
    vmem = pl.BlockSpec(memory_space=pltpu.VMEM)
    return pl.pallas_call(
        functools.partial(advance_kernel, n_case // 2, start),
        in_specs=[vmem] * 3,
        out_specs=vmem,
        out_shape=pltpu.VMEM((count, width), F32),
        compiler_params=pltpu.CompilerParams(vmem_limit_bytes=8 * 2**20),
        cost_estimate=pl.CostEstimate(
            flops=4 * count * rows * width, bytes_accessed=8 * count * width, transcendentals=0
        ),
        name="advance",
    )(*fd_parts, par)


def boundary_kernel(order, half, pick, *refs):
    pieces = refs[: len(order)]
    out_ref, hi, lo = refs[len(order) :]
    my_case = lax.axis_index("case")
    for mask, piece in zip(order, pieces):
        size = piece.shape[0]
        slot = lax.rem(my_case ^ mask, half)
        span = pl.ds(pl.multiple_of(slot * size, size), size)
        hi[span, :], lo[span, :] = split_hi_lo(piece[...])
    out_ref[...] = two_pass(hi[...], lo[...], pick[...])


def boundary_columns(order, pick, pieces, flops):
    cols, width = pick.shape
    total = sum(piece.shape[0] for piece in pieces)
    vmem = pl.BlockSpec(memory_space=pltpu.VMEM)
    return pl.pallas_call(
        functools.partial(boundary_kernel, order, len(order)),
        in_specs=[vmem] * (1 + len(pieces)),
        out_specs=vmem,
        out_shape=pltpu.VMEM((total, width), F32),
        scratch_shapes=[pltpu.VMEM((total, cols), BF16)] * 2,
        compiler_params=pltpu.CompilerParams(vmem_limit_bytes=8 * 2**20),
        cost_estimate=pl.CostEstimate(flops=flops, bytes_accessed=1, transcendentals=0),
        name="boundary_columns",
    )(pick, *pieces)


def relay_of_square(square, power, rate):
    return jnp.maximum(jnp.exp2(power * jnp.log2(square + 1e-4)) - 1.0, 0.0) * rate


def case_kernel(tie_ref, fault_ref, out_ref):
    out_ref[0:1, :] = tie_ref[...]
    out_ref[1:2, :] = fault_ref[...]


def case_rows(tie_x, fault_z):
    vmem = pl.BlockSpec(memory_space=pltpu.VMEM)
    return pl.pallas_call(
        case_kernel,
        in_specs=[vmem, vmem],
        out_specs=vmem,
        out_shape=pltpu.VMEM((2, tie_x.shape[1]), F32),
        compiler_params=pltpu.CompilerParams(vmem_limit_bytes=2**20),
        cost_estimate=pl.CostEstimate(flops=2**34, bytes_accessed=2**20, transcendentals=0),
        name="case_rows",
    )(tie_x, fault_z)


def branch_kernel(half, n_ahead, g_ref, far_ref, case_ref, par_ref, fd_ref, near_ref, far_edge_ref, *refs):
    ahead = refs[:n_ahead]
    volt_hbm, square_ref, worst_ref, vbuf, uh, ul, vsem = refs[n_ahead:]
    rows, cases = vbuf.shape
    branches = par_ref.shape[0]
    ext = uh.shape[0]
    g = g_ref[...] + far_ref[...]
    g1, g2, g3 = g[0:1], g[1:2], g[2:3]
    ratio = g2 / (case_ref[0:1, :] + g1)
    amps = 1.0 / (g3 - g2 * ratio + case_ref[1:2, :])

    def sag_of(fd):
        return (fd[:, :cases] - fd[:, cases:] * ratio) * amps

    side = lax.axis_index("case") // half
    for edge_ref, place in ((near_ref, side), (far_edge_ref, 1 - side)):
        size = edge_ref.shape[0]
        edge = pl.ds(pl.multiple_of(rows + place * size, size), size)
        uh[edge, :], ul[edge, :] = split_hi_lo(sag_of(edge_ref[...]))
    tiles = rows // TILE
    rim = rim_tile(half, tiles)
    for t in range(tiles):
        span = tile_span(rim + t, tiles)
        sag = sag_of(fd_ref[pl.ds(t * TILE, TILE), :])
        vbuf[span, :] = 1.0 - sag
        uh[span, :], ul[span, :] = split_hi_lo(sag)
    copy = pltpu.make_async_copy(vbuf, volt_hbm, vsem)
    copy.start()

    def drops(par, first):
        count = par.shape[0]
        bus = lax.broadcasted_iota(jnp.int32, (count, ext - first), 1) + first
        ends = incidence(bus.astype(F32), par)
        span = pl.ds(first, ext - first)
        return jnp.dot(ends, uh[span, :], preferred_element_type=F32) + jnp.dot(
            ends, ul[span, :], preferred_element_type=F32
        )

    def square_of(drop, par, start):
        scaled = drop * par[:, 2:3]
        square = scaled * scaled
        largest = square[:, :128]
        for c in range(128, cases, 128):
            largest = jnp.maximum(largest, square[:, c : c + 128])
        for h in range(par.shape[0] // 128):
            worst_ref[pl.ds(start // 128 + h, 1), :] = jnp.max(
                largest[h * 128 : (h + 1) * 128, :].T, axis=0, keepdims=True
            )
        return square

    def finish(drop, par, start):
        square_ref[pl.ds(start, par.shape[0]), :] = square_of(drop, par, start)

    starts = [sum(part.shape[0] for part in ahead[:i]) for i in range(n_ahead + 1)]
    whole = list(range(starts.pop(), branches, TILE))
    for n in range(max(len(whole), n_ahead)):
        if n < len(whole):
            par = par_ref[pl.ds(whole[n], TILE), :]
            finish(drops(par, 0), par, whole[n])
        if n < n_ahead:
            par = par_ref[pl.ds(starts[n], ahead[n].shape[0]), :]
            finish(sag_of(ahead[n][...]) + drops(par, rows), par, starts[n])
    copy.wait()


def screen_branches(g, g_far, case_par, par, fd, edges, ahead, n_case):
    count = case_par.shape[1]
    rows = fd.shape[0]
    branches = par.shape[0]
    ext = rows + sum(edge.shape[0] for edge in edges)
    vmem = pl.BlockSpec(memory_space=pltpu.VMEM)
    hbm = pl.BlockSpec(memory_space=pltpu.HBM)
    return pl.pallas_call(
        functools.partial(branch_kernel, n_case // 2, len(ahead)),
        in_specs=[vmem] * (7 + len(ahead)),
        out_specs=[hbm, vmem, vmem],
        out_shape=[
            jax.ShapeDtypeStruct((rows, count), F32),
            pltpu.VMEM((branches, count), F32),
            pltpu.VMEM((branches // 128, 128), F32),
        ],
        scratch_shapes=[
            pltpu.VMEM((rows, count), F32),
            pltpu.VMEM((ext, count), BF16),
            pltpu.VMEM((ext, count), BF16),
            pltpu.SemaphoreType.DMA,
        ],
        compiler_params=pltpu.CompilerParams(vmem_limit_bytes=24 * 2**20),
        name="screen_branches",
    )(g, g_far, case_par, par, fd, *edges, *ahead)


def relay_kernel(square_ref, par_ref, relay_hbm, rbuf, sems):
    rows = square_ref.shape[0]
    copies = []
    first = 0
    while first < rows:
        count = TILE if first + 2 * TILE <= rows else TILE // 2
        span = pl.ds(first, count)
        par = par_ref[span, :]
        rbuf[span, :] = relay_of_square(square_ref[span, :], par[:, 3:4], par[:, 4:5])
        sem = sems.at[len(copies)]
        copies.append(pltpu.make_async_copy(rbuf.at[span], relay_hbm.at[span], sem))
        copies[-1].start()
        first += count
    for copy in copies:
        copy.wait()


def relay_rates(square, par):
    rows = square.shape[0]
    vmem = pl.BlockSpec(memory_space=pltpu.VMEM)
    return pl.pallas_call(
        relay_kernel,
        in_specs=[vmem, vmem],
        out_specs=pl.BlockSpec(memory_space=pltpu.HBM),
        out_shape=jax.ShapeDtypeStruct(square.shape, F32),
        scratch_shapes=[
            pltpu.VMEM(square.shape, F32),
            pltpu.SemaphoreType.DMA((rows // TILE + 1,)),
        ],
        compiler_params=pltpu.CompilerParams(vmem_limit_bytes=8 * 2**20),
        cost_estimate=pl.CostEstimate(
            flops=8 * square.size, bytes_accessed=8 * square.size, transcendentals=2 * square.size
        ),
        name="relay_rates",
    )(square, par)


def per_device(
    z_columns,
    resident_bus,
    fault_col,
    switch_cols,
    tie_x,
    fault_z,
    boundary_send,
    branch_ends,
    branch_x,
    pickup,
    tds,
    curve,
):
    n_bus, n_case = lax.axis_size("bus"), lax.axis_size("case")
    half = n_case // 2
    fault, switch = fault_col[None], switch_cols.T
    send, z, pick = stage(z_columns, boundary_send, fault, switch, n_case)
    pairs = []
    for s in range(n_bus):
        for c in range(n_case):
            to = s + 1 if c < half else s - 1
            if 0 <= to < n_bus:
                pairs.append((s * n_case + c, to * n_case + c))
    own = lax.ppermute(send, ("bus", "case"), pairs)

    by_lines = [x.reshape(-1, 128) for x in (branch_x, pickup, tds, curve)]
    fd, g, par, *fd_parts = pick_columns(
        z,
        pick,
        fault,
        switch,
        resident_bus[None],
        z_columns,
        branch_ends.T,
        by_lines[:3],
        by_lines[3],
        n_case,
    )

    def swap_over_bus(g, bit):
        return lax.ppermute(g, "bus", [(i, i ^ bit) for i in range(n_bus)])

    def after(first, *values):
        return lax.optimization_barrier((first, *values))[1:]

    (own,) = after(g, own)
    other = lax.ppermute(own, "case", [(i, i ^ half) for i in range(n_case)])
    ahead = []
    sizes = [par.shape[0] // 12 * i for i in (3, 3)]
    bits = [2**i for i in range((n_bus - 1).bit_length())]
    for n, bit in enumerate(bits[:-1]):
        far = swap_over_bus(g, bit)
        if n == 1:
            (own,) = after(g, own)
        if n < len(sizes):
            ahead.append(advance(fd_parts, par, sum(sizes[:n]), sizes[n], n_case))
            (far,) = after(ahead[n], far)
        g = g + far
    g_far = swap_over_bus(g, bits[-1])
    (other,) = after(g, other)
    edges = []
    for piece, flops in ((own, 2**29), (other, 1)):
        pieces, order = [piece], [0]
        bit = half // 2
        while bit:
            swap = [(i, i ^ bit) for i in range(n_case)]
            pieces = pieces + [lax.ppermute(x, "case", swap) for x in pieces]
            order = order + [m ^ bit for m in order]
            bit //= 2
        edges.append(boundary_columns(order, pick, pieces, flops))
    voltage, square, worst = screen_branches(
        g, g_far, case_rows(tie_x[None], fault_z[None]), par, fd, edges, ahead, n_case
    )
    others = [
        lax.ppermute(worst, "case", [(i, i ^ m) for i in range(n_case)])
        for m in range(n_case - 1, 0, -1)
    ]
    relay_rate = relay_rates(square, par)
    half_power, factor = curve_constants(curve)
    worst = functools.reduce(jnp.maximum, others, worst).reshape(-1)
    worst_rate = relay_of_square(worst, half_power, 1.0 / (factor * tds))
    return (voltage, relay_rate, worst_rate)


def solution(mesh):
    in_specs = (
        P("bus", None),
        P(),
        P("case"),
        P("case", None),
        P("case"),
        P("case"),
        P(),
        P("bus", None),
        P("bus"),
        P("bus"),
        P("bus"),
        P("bus"),
    )
    out_specs = (P("bus", "case"), P("bus", "case"), P("bus"))
    return jax.shard_map(
        per_device, mesh=mesh, in_specs=in_specs, out_specs=out_specs, check_vma=False
    )
```

```python
import functools

import jax
import jax.numpy as jnp
from jax import lax
from jax.experimental import pallas as pl
from jax.experimental.pallas import tpu as pltpu
from jax.sharding import PartitionSpec as P

TILE = 256
STAGED = 2
F32 = jnp.float32
BF16 = jnp.bfloat16


def split_hi_lo(value):
    hi = value.astype(BF16)
    return hi, (value - hi.astype(F32)).astype(BF16)


def two_pass(hi, lo, rhs):
    return jnp.dot(hi, rhs, preferred_element_type=F32) + jnp.dot(
        lo, rhs, preferred_element_type=F32
    )


def in_hbm(*arrays):
    return [pltpu.with_memory_space_constraint(x, pltpu.HBM) for x in arrays]


def rim_tile(half, tiles):
    return (1 - lax.axis_index("case") // half) * (tiles - 1)


def tile_span(t, tiles):
    return pl.ds(pl.multiple_of(lax.rem(t, tiles) * TILE, TILE), TILE)


def stage_kernel(
    half, z_hbm, lists_hbm, fault_hbm, switch_hbm, send_ref, z_ref, pick_ref, lists, cases, sems
):
    tiles = z_hbm.shape[0] // TILE
    piece = send_ref.shape[0]
    my_bus, my_case = lax.axis_index("bus"), lax.axis_index("case")
    rim = rim_tile(half, tiles)
    loads = [
        pltpu.make_async_copy(fault_hbm, cases.at[pl.ds(0, 1)], sems.at[0]),
        pltpu.make_async_copy(switch_hbm, cases.at[pl.ds(8, 2)], sems.at[1]),
        pltpu.make_async_copy(lists_hbm.at[my_bus], lists, sems.at[2]),
    ]
    for t in range(z_ref.shape[0] // TILE):
        target = z_ref.at[pl.ds(t * TILE, TILE)]
        source = z_hbm.at[tile_span(rim + t, tiles)]
        loads.append(pltpu.make_async_copy(source, target, sems.at[3 + t]))
    for load in loads:
        load.start()
    for load in loads[:2]:
        load.wait()
    fill_picks(cases[0:1, :], cases[8:10, :], pick_ref)
    for load in loads[2:4]:
        load.wait()
    down = my_case // half
    base = (my_case % half) * piece
    first = rim * TILE
    for i in range(piece):
        row = jnp.clip(lists[1 - down, base + i] - first, 0, TILE - 1)
        send_ref[pl.ds(i, 1), :] = z_ref[pl.ds(row, 1), :]
    for load in loads[4:]:
        load.wait()


def stage(z_columns, boundary_send, fault, switch, n_case):
    cols = z_columns.shape[1]
    half = n_case // 2
    count = fault.shape[1]
    return pl.pallas_call(
        functools.partial(stage_kernel, half),
        in_specs=[pl.BlockSpec(memory_space=pltpu.HBM)] * 4,
        out_specs=[pl.BlockSpec(memory_space=pltpu.VMEM)] * 3,
        out_shape=[
            pltpu.VMEM((boundary_send.shape[2] // half, cols), F32),
            pltpu.VMEM((STAGED * TILE, cols), F32),
            pltpu.VMEM((cols, 2 * count), BF16),
        ],
        scratch_shapes=[
            pltpu.SMEM(boundary_send.shape[1:], jnp.int32),
            pltpu.VMEM((16, count), jnp.int32),
            pltpu.SemaphoreType.DMA((STAGED + 3,)),
        ],
        compiler_params=pltpu.CompilerParams(vmem_limit_bytes=4 * 2**20),
        name="stage",
    )(*in_hbm(z_columns, boundary_send, fault, switch))


def fill_picks(f, ab, pick):
    cols, count = pick.shape[0], f.shape[1]
    a, b = ab[0:1, :], ab[1:2, :]
    for t in range(cols // TILE):
        k = lax.broadcasted_iota(jnp.int32, (TILE, count), 0) + t * TILE
        span = pl.ds(t * TILE, TILE)
        pick[span, :count] = jnp.where(k == f, 1.0, 0.0).astype(BF16)
        pick[span, count:] = jnp.where(k == a, 1.0, jnp.where(k == b, -1.0, 0.0)).astype(BF16)


def columns_kernel(
    half,
    z_ref,
    pick,
    fault_ref,
    switch_ref,
    resident_ref,
    z_hbm,
    ends_hbm,
    x_hbm,
    pickup_hbm,
    tds_hbm,
    curve_hbm,
    fd_ref,
    g_ref,
    par_ref,
    fd_hi,
    fd_lo,
    later,
    ends,
    floats,
    curves,
    sems,
):
    rows, cols = z_hbm.shape
    cases = fault_ref.shape[1]
    tiles = rows // TILE
    rim = rim_tile(half, tiles)
    loads = []
    for t in range(STAGED, tiles):
        target = later.at[pl.ds((t - STAGED) * TILE, TILE)]
        source = z_hbm.at[tile_span(rim + t, tiles)]
        loads.append(pltpu.make_async_copy(source, target, sems.at[t]))
    small = [
        pltpu.make_async_copy(source, target, sems.at[tiles + i])
        for i, (source, target) in enumerate(
            [
                (ends_hbm, ends),
                (x_hbm, floats.at[0]),
                (pickup_hbm, floats.at[1]),
                (tds_hbm, floats.at[2]),
                (curve_hbm, curves),
            ]
        )
    ]
    for load in loads + small:
        load.start()
    f, a, b = fault_ref[...], switch_ref[0:1, :], switch_ref[1:2, :]
    resident = resident_ref[...] - lax.axis_index("bus") * rows
    g1 = jnp.zeros((1, cases), F32)
    g2 = jnp.zeros((1, cases), F32)
    g3 = jnp.zeros((1, cases), F32)
    k = lax.broadcasted_iota(jnp.int32, (TILE, cols), 1)
    for t in range(tiles + 1):
        if t == STAGED:
            for load in loads + small:
                load.wait()
        if t < tiles:
            if t < STAGED:
                z = z_ref[pl.ds(t * TILE, TILE), :]
            else:
                z = later[pl.ds((t - STAGED) * TILE, TILE), :]
            hi, lo = split_hi_lo(z)
            fd_ref[pl.ds(t * TILE, TILE), :] = two_pass(hi, lo, pick[...])
        if t == STAGED:
            gain = 1.0 / (floats[0] * floats[1])
            half_power, factor = curve_constants(curves[...])
            rate = 1.0 / (factor * floats[2])
            for c in range(gain.shape[0]):
                line = pl.ds(c * 128, 128)
                lines = [ends[:, line].astype(F32)]
                lines += [x[c : c + 1] for x in (gain, half_power, rate)]
                par_ref[line, :] = jnp.concatenate(lines + [jnp.zeros((3, 128), F32)]).T
        if t > 0:
            span = pl.ds((t - 1) * TILE, TILE)
            first = tile_span(rim + t - 1, tiles).start
            row = lax.broadcasted_iota(jnp.int32, (TILE, cols), 0) + first
            owner = jnp.max(jnp.where(row == resident, k, -1), axis=1, keepdims=True)
            fd_hi[span, :], fd_lo[span, :] = split_hi_lo(fd_ref[span, :])
            fault, diff = fd_ref[span, :cases], fd_ref[span, cases:]
            at_f = owner == f
            g3 += jnp.sum(jnp.where(at_f, fault, 0.0), axis=0, keepdims=True)
            g2 += jnp.sum(jnp.where(at_f, diff, 0.0), axis=0, keepdims=True)
            g1 += jnp.sum(
                jnp.where(owner == a, diff, jnp.where(owner == b, -diff, 0.0)),
                axis=0,
                keepdims=True,
            )
    g_ref[...] = jnp.concatenate([g1, g2, g3, jnp.zeros((g_ref.shape[0] - 3, cases), F32)])


def pick_columns(z, pick, fault, switch, resident, z_columns, ends, values, curve, n_case):
    rows, cols = z_columns.shape
    count = fault.shape[1]
    lines = curve.shape[0]
    vmem = pl.BlockSpec(memory_space=pltpu.VMEM)
    return pl.pallas_call(
        functools.partial(columns_kernel, n_case // 2),
        in_specs=[vmem] * 5 + [pl.BlockSpec(memory_space=pltpu.HBM)] * 6,
        out_specs=[vmem] * 5,
        out_shape=[
            pltpu.VMEM((rows, 2 * count), F32),
            pltpu.VMEM((4, count), F32),
            pltpu.VMEM((lines * 128, 8), F32),
            pltpu.VMEM((rows, 2 * count), BF16),
            pltpu.VMEM((rows, 2 * count), BF16),
        ],
        scratch_shapes=[
            pltpu.VMEM((rows - STAGED * TILE, cols), F32),
            pltpu.VMEM(ends.shape, jnp.int32),
            pltpu.VMEM((3, lines, 128), F32),
            pltpu.VMEM((lines, 128), jnp.int32),
            pltpu.SemaphoreType.DMA((rows // TILE + 5,)),
        ],
        compiler_params=pltpu.CompilerParams(vmem_limit_bytes=20 * 2**20),
        name="pick_columns",
    )(z, pick, fault, switch, resident, *in_hbm(z_columns, ends, *values, curve))


def curve_constants(curve):
    half_power = jnp.where(curve == 0, 0.01, jnp.where(curve == 1, 0.5, 1.0)).astype(F32)
    factor = jnp.where(curve == 0, 0.14, jnp.where(curve == 1, 13.5, 80.0)).astype(F32)
    return half_power, factor


def incidence(bus, par):
    return jnp.where(bus == par[:, 1:2], 1.0, jnp.where(bus == par[:, 0:1], -1.0, 0.0)).astype(BF16)


def advance_kernel(half, start, fd_hi, fd_lo, par_ref, out_ref):
    rows = fd_hi.shape[0]
    count = out_ref.shape[0]
    bus = lax.broadcasted_iota(jnp.int32, (count, rows), 1)
    bus = bus + rim_tile(half, rows // TILE) * TILE
    bus = jnp.where(bus >= rows, bus - rows, bus).astype(F32)
    ends = incidence(bus, par_ref[pl.ds(start, count), :])
    out_ref[...] = jnp.dot(ends, fd_hi[...], preferred_element_type=F32) + jnp.dot(
        ends, fd_lo[...], preferred_element_type=F32
    )


def advance(fd_parts, par, start, count, n_case):
    rows, width = fd_parts[0].shape
    vmem = pl.BlockSpec(memory_space=pltpu.VMEM)
    return pl.pallas_call(
        functools.partial(advance_kernel, n_case // 2, start),
        in_specs=[vmem] * 3,
        out_specs=vmem,
        out_shape=pltpu.VMEM((count, width), F32),
        compiler_params=pltpu.CompilerParams(vmem_limit_bytes=8 * 2**20),
        cost_estimate=pl.CostEstimate(
            flops=4 * count * rows * width, bytes_accessed=8 * count * width, transcendentals=0
        ),
        name="advance",
    )(*fd_parts, par)


def boundary_kernel(order, half, pick, *refs):
    pieces = refs[: len(order)]
    out_ref, hi, lo = refs[len(order) :]
    my_case = lax.axis_index("case")
    for mask, piece in zip(order, pieces):
        size = piece.shape[0]
        slot = lax.rem(my_case ^ mask, half)
        span = pl.ds(pl.multiple_of(slot * size, size), size)
        hi[span, :], lo[span, :] = split_hi_lo(piece[...])
    out_ref[...] = two_pass(hi[...], lo[...], pick[...])


def boundary_columns(order, pick, pieces, flops):
    cols, width = pick.shape
    total = sum(piece.shape[0] for piece in pieces)
    vmem = pl.BlockSpec(memory_space=pltpu.VMEM)
    return pl.pallas_call(
        functools.partial(boundary_kernel, order, len(order)),
        in_specs=[vmem] * (1 + len(pieces)),
        out_specs=vmem,
        out_shape=pltpu.VMEM((total, width), F32),
        scratch_shapes=[pltpu.VMEM((total, cols), BF16)] * 2,
        compiler_params=pltpu.CompilerParams(vmem_limit_bytes=8 * 2**20),
        cost_estimate=pl.CostEstimate(flops=flops, bytes_accessed=1, transcendentals=0),
        name="boundary_columns",
    )(pick, *pieces)


def relay_of_square(square, power, rate):
    return jnp.maximum(jnp.exp2(power * jnp.log2(square + 1e-4)) - 1.0, 0.0) * rate


def case_kernel(tie_ref, fault_ref, out_ref):
    out_ref[0:1, :] = tie_ref[...]
    out_ref[1:2, :] = fault_ref[...]


def case_rows(tie_x, fault_z):
    vmem = pl.BlockSpec(memory_space=pltpu.VMEM)
    return pl.pallas_call(
        case_kernel,
        in_specs=[vmem, vmem],
        out_specs=vmem,
        out_shape=pltpu.VMEM((2, tie_x.shape[1]), F32),
        compiler_params=pltpu.CompilerParams(vmem_limit_bytes=2**20),
        cost_estimate=pl.CostEstimate(flops=2**34, bytes_accessed=2**20, transcendentals=0),
        name="case_rows",
    )(tie_x, fault_z)


def branch_kernel(half, n_ahead, g_ref, far_ref, case_ref, par_ref, fd_ref, near_ref, far_edge_ref, *refs):
    ahead = refs[:n_ahead]
    volt_hbm, square_ref, rate_ref, worst_ref, vbuf, uh, ul, vsem = refs[n_ahead:]
    rows, cases = vbuf.shape
    branches = par_ref.shape[0]
    ext = uh.shape[0]
    g = g_ref[...] + far_ref[...]
    g1, g2, g3 = g[0:1], g[1:2], g[2:3]
    ratio = g2 / (case_ref[0:1, :] + g1)
    amps = 1.0 / (g3 - g2 * ratio + case_ref[1:2, :])

    def sag_of(fd):
        return (fd[:, :cases] - fd[:, cases:] * ratio) * amps

    side = lax.axis_index("case") // half
    for edge_ref, place in ((near_ref, side), (far_edge_ref, 1 - side)):
        size = edge_ref.shape[0]
        edge = pl.ds(pl.multiple_of(rows + place * size, size), size)
        uh[edge, :], ul[edge, :] = split_hi_lo(sag_of(edge_ref[...]))
    tiles = rows // TILE
    rim = rim_tile(half, tiles)
    for t in range(tiles):
        span = tile_span(rim + t, tiles)
        sag = sag_of(fd_ref[pl.ds(t * TILE, TILE), :])
        vbuf[span, :] = 1.0 - sag
        uh[span, :], ul[span, :] = split_hi_lo(sag)
    copy = pltpu.make_async_copy(vbuf, volt_hbm, vsem)
    copy.start()

    def drops(par, first):
        count = par.shape[0]
        bus = lax.broadcasted_iota(jnp.int32, (count, ext - first), 1) + first
        ends = incidence(bus.astype(F32), par)
        span = pl.ds(first, ext - first)
        return jnp.dot(ends, uh[span, :], preferred_element_type=F32) + jnp.dot(
            ends, ul[span, :], preferred_element_type=F32
        )

    def square_of(drop, par, start):
        scaled = drop * par[:, 2:3]
        square = scaled * scaled
        largest = square[:, :128]
        for c in range(128, cases, 128):
            largest = jnp.maximum(largest, square[:, c : c + 128])
        for h in range(par.shape[0] // 128):
            worst_ref[pl.ds(start // 128 + h, 1), :] = jnp.max(
                largest[h * 128 : (h + 1) * 128, :].T, axis=0, keepdims=True
            )
        return square

    later = square_ref.shape[0]

    def finish(drop, par, start):
        square = square_of(drop, par, start)
        if start < later:
            square_ref[pl.ds(start, par.shape[0]), :] = square
        else:
            rate = relay_of_square(square, par[:, 3:4], par[:, 4:5])
            rate_ref[pl.ds(start - later, par.shape[0]), :] = rate

    starts = [sum(part.shape[0] for part in ahead[:i]) for i in range(n_ahead + 1)]
    whole = list(range(starts.pop(), branches, TILE))
    for n in range(max(len(whole), n_ahead)):
        if n < len(whole):
            par = par_ref[pl.ds(whole[n], TILE), :]
            finish(drops(par, 0), par, whole[n])
        if n < n_ahead:
            par = par_ref[pl.ds(starts[n], ahead[n].shape[0]), :]
            finish(sag_of(ahead[n][...]) + drops(par, rows), par, starts[n])
    copy.wait()


def screen_branches(g, g_far, case_par, par, fd, edges, ahead, n_case):
    count = case_par.shape[1]
    rows = fd.shape[0]
    branches = par.shape[0]
    ext = rows + sum(edge.shape[0] for edge in edges)
    later = sum(part.shape[0] for part in ahead)
    vmem = pl.BlockSpec(memory_space=pltpu.VMEM)
    hbm = pl.BlockSpec(memory_space=pltpu.HBM)
    return pl.pallas_call(
        functools.partial(branch_kernel, n_case // 2, len(ahead)),
        in_specs=[vmem] * (7 + len(ahead)),
        out_specs=[hbm, vmem, vmem, vmem],
        out_shape=[
            jax.ShapeDtypeStruct((rows, count), F32),
            pltpu.VMEM((later, count), F32),
            pltpu.VMEM((branches - later, count), F32),
            pltpu.VMEM((branches // 128, 128), F32),
        ],
        scratch_shapes=[
            pltpu.VMEM((rows, count), F32),
            pltpu.VMEM((ext, count), BF16),
            pltpu.VMEM((ext, count), BF16),
            pltpu.SemaphoreType.DMA,
        ],
        compiler_params=pltpu.CompilerParams(vmem_limit_bytes=24 * 2**20),
        name="screen_branches",
    )(g, g_far, case_par, par, fd, *edges, *ahead)


def relay_kernel(square_ref, rate_ref, par_ref, relay_hbm, rbuf, sems):
    rows = square_ref.shape[0]
    target = relay_hbm.at[pl.ds(rows, rate_ref.shape[0])]
    copies = [pltpu.make_async_copy(rate_ref, target, sems.at[0])]
    copies[0].start()
    first = 0
    while first < rows:
        count = TILE if first + 2 * TILE <= rows else TILE // 2
        span = pl.ds(first, count)
        par = par_ref[span, :]
        rbuf[span, :] = relay_of_square(square_ref[span, :], par[:, 3:4], par[:, 4:5])
        sem = sems.at[len(copies)]
        copies.append(pltpu.make_async_copy(rbuf.at[span], relay_hbm.at[span], sem))
        copies[-1].start()
        first += count
    for copy in copies:
        copy.wait()


def relay_rates(square, rate, par):
    rows, count = square.shape
    vmem = pl.BlockSpec(memory_space=pltpu.VMEM)
    return pl.pallas_call(
        relay_kernel,
        in_specs=[vmem, vmem, vmem],
        out_specs=pl.BlockSpec(memory_space=pltpu.HBM),
        out_shape=jax.ShapeDtypeStruct((rows + rate.shape[0], count), F32),
        scratch_shapes=[
            pltpu.VMEM(square.shape, F32),
            pltpu.SemaphoreType.DMA((rows // TILE + 2,)),
        ],
        compiler_params=pltpu.CompilerParams(vmem_limit_bytes=8 * 2**20),
        cost_estimate=pl.CostEstimate(
            flops=8 * square.size, bytes_accessed=8 * square.size, transcendentals=2 * square.size
        ),
        name="relay_rates",
    )(square, rate, par)


def per_device(
    z_columns,
    resident_bus,
    fault_col,
    switch_cols,
    tie_x,
    fault_z,
    boundary_send,
    branch_ends,
    branch_x,
    pickup,
    tds,
    curve,
):
    n_bus, n_case = lax.axis_size("bus"), lax.axis_size("case")
    half = n_case // 2
    fault, switch = fault_col[None], switch_cols.T
    send, z, pick = stage(z_columns, boundary_send, fault, switch, n_case)
    pairs = []
    for s in range(n_bus):
        for c in range(n_case):
            to = s + 1 if c < half else s - 1
            if 0 <= to < n_bus:
                pairs.append((s * n_case + c, to * n_case + c))
    own = lax.ppermute(send, ("bus", "case"), pairs)

    by_lines = [x.reshape(-1, 128) for x in (branch_x, pickup, tds, curve)]
    fd, g, par, *fd_parts = pick_columns(
        z,
        pick,
        fault,
        switch,
        resident_bus[None],
        z_columns,
        branch_ends.T,
        by_lines[:3],
        by_lines[3],
        n_case,
    )

    def swap_over_bus(g, bit):
        return lax.ppermute(g, "bus", [(i, i ^ bit) for i in range(n_bus)])

    def after(first, *values):
        return lax.optimization_barrier((first, *values))[1:]

    (own,) = after(g, own)
    other = lax.ppermute(own, "case", [(i, i ^ half) for i in range(n_case)])
    ahead = []
    sizes = [par.shape[0] // 12 * i for i in (3, 3)]
    bits = [2**i for i in range((n_bus - 1).bit_length())]
    for n, bit in enumerate(bits[:-1]):
        far = swap_over_bus(g, bit)
        if n == 1:
            (own,) = after(g, own)
        if n < len(sizes):
            ahead.append(advance(fd_parts, par, sum(sizes[:n]), sizes[n], n_case))
            (far,) = after(ahead[n], far)
        g = g + far
    g_far = swap_over_bus(g, bits[-1])
    (other,) = after(g, other)
    edges = []
    for piece, flops in ((own, 2**29), (other, 1)):
        pieces, order = [piece], [0]
        bit = half // 2
        while bit:
            swap = [(i, i ^ bit) for i in range(n_case)]
            pieces = pieces + [lax.ppermute(x, "case", swap) for x in pieces]
            order = order + [m ^ bit for m in order]
            bit //= 2
        edges.append(boundary_columns(order, pick, pieces, flops))
    voltage, square, rate, worst = screen_branches(
        g, g_far, case_rows(tie_x[None], fault_z[None]), par, fd, edges, ahead, n_case
    )
    others = [
        lax.ppermute(worst, "case", [(i, i ^ m) for i in range(n_case)])
        for m in range(n_case - 1, 0, -1)
    ]
    relay_rate = relay_rates(square, rate, par)
    half_power, factor = curve_constants(curve)
    worst = functools.reduce(jnp.maximum, others, worst).reshape(-1)
    worst_rate = relay_of_square(worst, half_power, 1.0 / (factor * tds))
    return (voltage, relay_rate, worst_rate)


def solution(mesh):
    in_specs = (
        P("bus", None),
        P(),
        P("case"),
        P("case", None),
        P("case"),
        P("case"),
        P(),
        P("bus", None),
        P("bus"),
        P("bus"),
        P("bus"),
        P("bus"),
    )
    out_specs = (P("bus", "case"), P("bus", "case"), P("bus"))
    return jax.shard_map(
        per_device, mesh=mesh, in_specs=in_specs, out_specs=out_specs, check_vma=False
    )
```

```python
import functools

import jax
import jax.numpy as jnp
from jax import lax
from jax.experimental import pallas as pl
from jax.experimental.pallas import tpu as pltpu
from jax.sharding import PartitionSpec as P

TILE = 256
STAGED = 2
F32 = jnp.float32
BF16 = jnp.bfloat16


def split_hi_lo(value):
    hi = value.astype(BF16)
    return hi, (value - hi.astype(F32)).astype(BF16)


def two_pass(hi, lo, rhs):
    return jnp.dot(hi, rhs, preferred_element_type=F32) + jnp.dot(
        lo, rhs, preferred_element_type=F32
    )


def in_hbm(*arrays):
    return [pltpu.with_memory_space_constraint(x, pltpu.HBM) for x in arrays]


def rim_tile(half, tiles):
    return (1 - lax.axis_index("case") // half) * (tiles - 1)


def tile_span(t, tiles):
    return pl.ds(pl.multiple_of(lax.rem(t, tiles) * TILE, TILE), TILE)


def stage_kernel(
    half, z_hbm, lists_hbm, fault_hbm, switch_hbm, send_ref, z_ref, pick_ref, lists, cases, sems
):
    tiles = z_hbm.shape[0] // TILE
    piece = send_ref.shape[0]
    my_bus, my_case = lax.axis_index("bus"), lax.axis_index("case")
    rim = rim_tile(half, tiles)
    loads = [
        pltpu.make_async_copy(fault_hbm, cases.at[pl.ds(0, 1)], sems.at[0]),
        pltpu.make_async_copy(switch_hbm, cases.at[pl.ds(8, 2)], sems.at[1]),
        pltpu.make_async_copy(lists_hbm.at[my_bus], lists, sems.at[2]),
    ]
    for t in range(z_ref.shape[0] // TILE):
        target = z_ref.at[pl.ds(t * TILE, TILE)]
        source = z_hbm.at[tile_span(rim + t, tiles)]
        loads.append(pltpu.make_async_copy(source, target, sems.at[3 + t]))
    for load in loads:
        load.start()
    for load in loads[:2]:
        load.wait()
    fill_picks(cases[0:1, :], cases[8:10, :], pick_ref)
    for load in loads[2:4]:
        load.wait()
    down = my_case // half
    base = (my_case % half) * piece
    first = rim * TILE
    for i in range(piece):
        row = jnp.clip(lists[1 - down, base + i] - first, 0, TILE - 1)
        send_ref[pl.ds(i, 1), :] = z_ref[pl.ds(row, 1), :]
    for load in loads[4:]:
        load.wait()


def stage(z_columns, boundary_send, fault, switch, n_case):
    cols = z_columns.shape[1]
    half = n_case // 2
    count = fault.shape[1]
    return pl.pallas_call(
        functools.partial(stage_kernel, half),
        in_specs=[pl.BlockSpec(memory_space=pltpu.HBM)] * 4,
        out_specs=[pl.BlockSpec(memory_space=pltpu.VMEM)] * 3,
        out_shape=[
            pltpu.VMEM((boundary_send.shape[2] // half, cols), F32),
            pltpu.VMEM((STAGED * TILE, cols), F32),
            pltpu.VMEM((cols, 2 * count), BF16),
        ],
        scratch_shapes=[
            pltpu.SMEM(boundary_send.shape[1:], jnp.int32),
            pltpu.VMEM((16, count), jnp.int32),
            pltpu.SemaphoreType.DMA((STAGED + 3,)),
        ],
        compiler_params=pltpu.CompilerParams(vmem_limit_bytes=4 * 2**20),
        name="stage",
    )(*in_hbm(z_columns, boundary_send, fault, switch))


def fill_picks(f, ab, pick):
    cols, count = pick.shape[0], f.shape[1]
    a, b = ab[0:1, :], ab[1:2, :]
    for t in range(cols // TILE):
        k = lax.broadcasted_iota(jnp.int32, (TILE, count), 0) + t * TILE
        span = pl.ds(t * TILE, TILE)
        pick[span, :count] = jnp.where(k == f, 1.0, 0.0).astype(BF16)
        pick[span, count:] = jnp.where(k == a, 1.0, jnp.where(k == b, -1.0, 0.0)).astype(BF16)


def columns_kernel(
    half,
    z_ref,
    pick,
    fault_ref,
    switch_ref,
    resident_ref,
    z_hbm,
    ends_hbm,
    x_hbm,
    pickup_hbm,
    tds_hbm,
    curve_hbm,
    fd_ref,
    g_ref,
    par_ref,
    fd_hi,
    fd_lo,
    later,
    ends,
    floats,
    curves,
    sems,
):
    rows, cols = z_hbm.shape
    cases = fault_ref.shape[1]
    tiles = rows // TILE
    rim = rim_tile(half, tiles)
    loads = []
    for t in range(STAGED, tiles):
        target = later.at[pl.ds((t - STAGED) * TILE, TILE)]
        source = z_hbm.at[tile_span(rim + t, tiles)]
        loads.append(pltpu.make_async_copy(source, target, sems.at[t]))
    small = [
        pltpu.make_async_copy(source, target, sems.at[tiles + i])
        for i, (source, target) in enumerate(
            [
                (ends_hbm, ends),
                (x_hbm, floats.at[0]),
                (pickup_hbm, floats.at[1]),
                (tds_hbm, floats.at[2]),
                (curve_hbm, curves),
            ]
        )
    ]
    for load in loads + small:
        load.start()
    f, a, b = fault_ref[...], switch_ref[0:1, :], switch_ref[1:2, :]
    resident = resident_ref[...] - lax.axis_index("bus") * rows
    g1 = jnp.zeros((1, cases), F32)
    g2 = jnp.zeros((1, cases), F32)
    g3 = jnp.zeros((1, cases), F32)
    k = lax.broadcasted_iota(jnp.int32, (TILE, cols), 1)
    for t in range(tiles + 1):
        if t == STAGED:
            for load in loads + small:
                load.wait()
        if t < tiles:
            if t < STAGED:
                z = z_ref[pl.ds(t * TILE, TILE), :]
            else:
                z = later[pl.ds((t - STAGED) * TILE, TILE), :]
            hi, lo = split_hi_lo(z)
            fd_ref[pl.ds(t * TILE, TILE), :] = two_pass(hi, lo, pick[...])
        if t == STAGED:
            gain = 1.0 / (floats[0] * floats[1])
            half_power, factor = curve_constants(curves[...])
            rate = 1.0 / (factor * floats[2])
            for c in range(gain.shape[0]):
                line = pl.ds(c * 128, 128)
                lines = [ends[:, line].astype(F32)]
                lines += [x[c : c + 1] for x in (gain, half_power, rate)]
                par_ref[line, :] = jnp.concatenate(lines + [jnp.zeros((3, 128), F32)]).T
        if t > 0:
            span = pl.ds((t - 1) * TILE, TILE)
            first = tile_span(rim + t - 1, tiles).start
            row = lax.broadcasted_iota(jnp.int32, (TILE, cols), 0) + first
            owner = jnp.max(jnp.where(row == resident, k, -1), axis=1, keepdims=True)
            fd_hi[span, :], fd_lo[span, :] = split_hi_lo(fd_ref[span, :])
            fault, diff = fd_ref[span, :cases], fd_ref[span, cases:]
            at_f = owner == f
            g3 += jnp.sum(jnp.where(at_f, fault, 0.0), axis=0, keepdims=True)
            g2 += jnp.sum(jnp.where(at_f, diff, 0.0), axis=0, keepdims=True)
            g1 += jnp.sum(
                jnp.where(owner == a, diff, jnp.where(owner == b, -diff, 0.0)),
                axis=0,
                keepdims=True,
            )
    g_ref[...] = jnp.concatenate([g1, g2, g3, jnp.zeros((g_ref.shape[0] - 3, cases), F32)])


def pick_columns(z, pick, fault, switch, resident, z_columns, ends, values, curve, n_case):
    rows, cols = z_columns.shape
    count = fault.shape[1]
    lines = curve.shape[0]
    vmem = pl.BlockSpec(memory_space=pltpu.VMEM)
    return pl.pallas_call(
        functools.partial(columns_kernel, n_case // 2),
        in_specs=[vmem] * 5 + [pl.BlockSpec(memory_space=pltpu.HBM)] * 6,
        out_specs=[vmem] * 5,
        out_shape=[
            pltpu.VMEM((rows, 2 * count), F32),
            pltpu.VMEM((4, count), F32),
            pltpu.VMEM((lines * 128, 8), F32),
            pltpu.VMEM((rows, 2 * count), BF16),
            pltpu.VMEM((rows, 2 * count), BF16),
        ],
        scratch_shapes=[
            pltpu.VMEM((rows - STAGED * TILE, cols), F32),
            pltpu.VMEM(ends.shape, jnp.int32),
            pltpu.VMEM((3, lines, 128), F32),
            pltpu.VMEM((lines, 128), jnp.int32),
            pltpu.SemaphoreType.DMA((rows // TILE + 5,)),
        ],
        compiler_params=pltpu.CompilerParams(vmem_limit_bytes=20 * 2**20),
        name="pick_columns",
    )(z, pick, fault, switch, resident, *in_hbm(z_columns, ends, *values, curve))


def curve_constants(curve):
    half_power = jnp.where(curve == 0, 0.01, jnp.where(curve == 1, 0.5, 1.0)).astype(F32)
    factor = jnp.where(curve == 0, 0.14, jnp.where(curve == 1, 13.5, 80.0)).astype(F32)
    return half_power, factor


def incidence(bus, par):
    return jnp.where(bus == par[:, 1:2], 1.0, jnp.where(bus == par[:, 0:1], -1.0, 0.0)).astype(BF16)


def advance_kernel(half, start, fd_hi, fd_lo, par_ref, out_ref):
    rows = fd_hi.shape[0]
    count = out_ref.shape[0]
    bus = lax.broadcasted_iota(jnp.int32, (count, rows), 1)
    bus = bus + rim_tile(half, rows // TILE) * TILE
    bus = jnp.where(bus >= rows, bus - rows, bus).astype(F32)
    ends = incidence(bus, par_ref[pl.ds(start, count), :])
    out_ref[...] = jnp.dot(ends, fd_hi[...], preferred_element_type=F32) + jnp.dot(
        ends, fd_lo[...], preferred_element_type=F32
    )


def advance(fd_parts, par, start, count, n_case):
    rows, width = fd_parts[0].shape
    vmem = pl.BlockSpec(memory_space=pltpu.VMEM)
    return pl.pallas_call(
        functools.partial(advance_kernel, n_case // 2, start),
        in_specs=[vmem] * 3,
        out_specs=vmem,
        out_shape=pltpu.VMEM((count, width), F32),
        compiler_params=pltpu.CompilerParams(vmem_limit_bytes=8 * 2**20),
        cost_estimate=pl.CostEstimate(
            flops=4 * count * rows * width, bytes_accessed=8 * count * width, transcendentals=0
        ),
        name="advance",
    )(*fd_parts, par)


def boundary_kernel(order, half, pick, *refs):
    pieces = refs[: len(order)]
    out_ref, hi, lo = refs[len(order) :]
    my_case = lax.axis_index("case")
    for mask, piece in zip(order, pieces):
        size = piece.shape[0]
        slot = lax.rem(my_case ^ mask, half)
        span = pl.ds(pl.multiple_of(slot * size, size), size)
        hi[span, :], lo[span, :] = split_hi_lo(piece[...])
    out_ref[...] = two_pass(hi[...], lo[...], pick[...])


def boundary_columns(order, pick, pieces, flops):
    cols, width = pick.shape
    total = sum(piece.shape[0] for piece in pieces)
    vmem = pl.BlockSpec(memory_space=pltpu.VMEM)
    return pl.pallas_call(
        functools.partial(boundary_kernel, order, len(order)),
        in_specs=[vmem] * (1 + len(pieces)),
        out_specs=vmem,
        out_shape=pltpu.VMEM((total, width), F32),
        scratch_shapes=[pltpu.VMEM((total, cols), BF16)] * 2,
        compiler_params=pltpu.CompilerParams(vmem_limit_bytes=8 * 2**20),
        cost_estimate=pl.CostEstimate(flops=flops, bytes_accessed=1, transcendentals=0),
        name="boundary_columns",
    )(pick, *pieces)


def relay_of_square(square, power, rate):
    return jnp.maximum(jnp.exp2(power * jnp.log2(square + 1e-4)) - 1.0, 0.0) * rate


def case_kernel(tie_ref, fault_ref, out_ref):
    out_ref[0:1, :] = tie_ref[...]
    out_ref[1:2, :] = fault_ref[...]


def case_rows(tie_x, fault_z):
    vmem = pl.BlockSpec(memory_space=pltpu.VMEM)
    return pl.pallas_call(
        case_kernel,
        in_specs=[vmem, vmem],
        out_specs=vmem,
        out_shape=pltpu.VMEM((2, tie_x.shape[1]), F32),
        compiler_params=pltpu.CompilerParams(vmem_limit_bytes=2**20),
        cost_estimate=pl.CostEstimate(flops=2**34, bytes_accessed=2**20, transcendentals=0),
        name="case_rows",
    )(tie_x, fault_z)


def branch_kernel(half, n_ahead, g_ref, far_ref, case_ref, par_ref, fd_ref, near_ref, far_edge_ref, *refs):
    ahead = refs[:n_ahead]
    volt_hbm, square_ref, rate_ref, worst_ref, vbuf, uh, ul, vsem = refs[n_ahead:]
    rows, cases = vbuf.shape
    branches = par_ref.shape[0]
    ext = uh.shape[0]
    g = g_ref[...] + far_ref[...]
    g1, g2, g3 = g[0:1], g[1:2], g[2:3]
    ratio = g2 / (case_ref[0:1, :] + g1)
    amps = 1.0 / (g3 - g2 * ratio + case_ref[1:2, :])

    def sag_of(fd):
        return (fd[:, :cases] - fd[:, cases:] * ratio) * amps

    side = lax.axis_index("case") // half
    for edge_ref, place in ((near_ref, side), (far_edge_ref, 1 - side)):
        size = edge_ref.shape[0]
        edge = pl.ds(pl.multiple_of(rows + place * size, size), size)
        uh[edge, :], ul[edge, :] = split_hi_lo(sag_of(edge_ref[...]))
    tiles = rows // TILE
    rim = rim_tile(half, tiles)
    for t in range(tiles):
        span = tile_span(rim + t, tiles)
        sag = sag_of(fd_ref[pl.ds(t * TILE, TILE), :])
        vbuf[span, :] = 1.0 - sag
        uh[span, :], ul[span, :] = split_hi_lo(sag)
    copy = pltpu.make_async_copy(vbuf, volt_hbm, vsem)
    copy.start()

    def drops(par, first):
        count = par.shape[0]
        bus = lax.broadcasted_iota(jnp.int32, (count, ext - first), 1) + first
        ends = incidence(bus.astype(F32), par)
        span = pl.ds(first, ext - first)
        return jnp.dot(ends, uh[span, :], preferred_element_type=F32) + jnp.dot(
            ends, ul[span, :], preferred_element_type=F32
        )

    def square_of(drop, par, start):
        scaled = drop * par[:, 2:3]
        square = scaled * scaled
        largest = square[:, :128]
        for c in range(128, cases, 128):
            largest = jnp.maximum(largest, square[:, c : c + 128])
        for h in range(par.shape[0] // 128):
            worst_ref[pl.ds(start // 128 + h, 1), :] = jnp.max(
                largest[h * 128 : (h + 1) * 128, :].T, axis=0, keepdims=True
            )
        return square

    later = square_ref.shape[0]

    def finish(drop, par, start):
        square = square_of(drop, par, start)
        if start < later:
            square_ref[pl.ds(start, par.shape[0]), :] = square
        else:
            rate = relay_of_square(square, par[:, 3:4], par[:, 4:5])
            rate_ref[pl.ds(start - later, par.shape[0]), :] = rate

    starts = [sum(part.shape[0] for part in ahead[:i]) for i in range(n_ahead + 1)]
    whole = list(range(starts.pop(), branches, TILE))
    for n in range(max(len(whole), n_ahead)):
        if n < len(whole):
            par = par_ref[pl.ds(whole[n], TILE), :]
            finish(drops(par, 0), par, whole[n])
        if n < n_ahead:
            par = par_ref[pl.ds(starts[n], ahead[n].shape[0]), :]
            finish(sag_of(ahead[n][...]) + drops(par, rows), par, starts[n])
    copy.wait()


def screen_branches(g, g_far, case_par, par, fd, edges, ahead, n_case):
    count = case_par.shape[1]
    rows = fd.shape[0]
    branches = par.shape[0]
    ext = rows + sum(edge.shape[0] for edge in edges)
    later = sum(part.shape[0] for part in ahead)
    vmem = pl.BlockSpec(memory_space=pltpu.VMEM)
    hbm = pl.BlockSpec(memory_space=pltpu.HBM)
    return pl.pallas_call(
        functools.partial(branch_kernel, n_case // 2, len(ahead)),
        in_specs=[vmem] * (7 + len(ahead)),
        out_specs=[hbm, vmem, vmem, vmem],
        out_shape=[
            jax.ShapeDtypeStruct((rows, count), F32),
            pltpu.VMEM((later, count), F32),
            pltpu.VMEM((branches - later, count), F32),
            pltpu.VMEM((branches // 128, 128), F32),
        ],
        scratch_shapes=[
            pltpu.VMEM((rows, count), F32),
            pltpu.VMEM((ext, count), BF16),
            pltpu.VMEM((ext, count), BF16),
            pltpu.SemaphoreType.DMA,
        ],
        compiler_params=pltpu.CompilerParams(vmem_limit_bytes=24 * 2**20),
        name="screen_branches",
    )(g, g_far, case_par, par, fd, *edges, *ahead)


def relay_kernel(square_ref, rate_ref, par_ref, relay_hbm, rbuf, sems):
    rows = square_ref.shape[0]
    target = relay_hbm.at[pl.ds(rows, rate_ref.shape[0])]
    copies = [pltpu.make_async_copy(rate_ref, target, sems.at[0])]
    copies[0].start()
    first = 0
    while first < rows:
        count = TILE if first + 2 * TILE <= rows else TILE // 2
        span = pl.ds(first, count)
        par = par_ref[span, :]
        rbuf[span, :] = relay_of_square(square_ref[span, :], par[:, 3:4], par[:, 4:5])
        sem = sems.at[len(copies)]
        copies.append(pltpu.make_async_copy(rbuf.at[span], relay_hbm.at[span], sem))
        copies[-1].start()
        first += count
    for copy in copies:
        copy.wait()


def relay_rates(square, rate, par):
    rows, count = square.shape
    vmem = pl.BlockSpec(memory_space=pltpu.VMEM)
    return pl.pallas_call(
        relay_kernel,
        in_specs=[vmem, vmem, vmem],
        out_specs=pl.BlockSpec(memory_space=pltpu.HBM),
        out_shape=jax.ShapeDtypeStruct((rows + rate.shape[0], count), F32),
        scratch_shapes=[
            pltpu.VMEM(square.shape, F32),
            pltpu.SemaphoreType.DMA((rows // TILE + 2,)),
        ],
        compiler_params=pltpu.CompilerParams(vmem_limit_bytes=8 * 2**20),
        cost_estimate=pl.CostEstimate(
            flops=8 * square.size, bytes_accessed=8 * square.size, transcendentals=2 * square.size
        ),
        name="relay_rates",
    )(square, rate, par)


def per_device(
    z_columns,
    resident_bus,
    fault_col,
    switch_cols,
    tie_x,
    fault_z,
    boundary_send,
    branch_ends,
    branch_x,
    pickup,
    tds,
    curve,
):
    n_bus, n_case = lax.axis_size("bus"), lax.axis_size("case")
    half = n_case // 2
    fault, switch = fault_col[None], switch_cols.T
    send, z, pick = stage(z_columns, boundary_send, fault, switch, n_case)
    pairs = []
    for s in range(n_bus):
        for c in range(n_case):
            to = s + 1 if c < half else s - 1
            if 0 <= to < n_bus:
                pairs.append((s * n_case + c, to * n_case + c))
    own = lax.ppermute(send, ("bus", "case"), pairs)

    by_lines = [x.reshape(-1, 128) for x in (branch_x, pickup, tds, curve)]
    fd, g, par, *fd_parts = pick_columns(
        z,
        pick,
        fault,
        switch,
        resident_bus[None],
        z_columns,
        branch_ends.T,
        by_lines[:3],
        by_lines[3],
        n_case,
    )

    def swap_over_bus(g, bit):
        return lax.ppermute(g, "bus", [(i, i ^ bit) for i in range(n_bus)])

    def after(first, *values):
        return lax.optimization_barrier((first, *values))[1:]

    (own,) = after(g, own)
    other = lax.ppermute(own, "case", [(i, i ^ half) for i in range(n_case)])
    ahead = []
    sizes = [par.shape[0] // 12 * i for i in (2, 4)]
    bits = [2**i for i in range((n_bus - 1).bit_length())]
    for n, bit in enumerate(bits[:-1]):
        far = swap_over_bus(g, bit)
        if n == 1:
            (own,) = after(g, own)
        if n < len(sizes):
            ahead.append(advance(fd_parts, par, sum(sizes[:n]), sizes[n], n_case))
            (far,) = after(ahead[n], far)
        g = g + far
    g_far = swap_over_bus(g, bits[-1])
    (other,) = after(g, other)
    edges = []
    for piece, flops in ((own, 2**29), (other, 1)):
        pieces, order = [piece], [0]
        bit = half // 2
        while bit:
            swap = [(i, i ^ bit) for i in range(n_case)]
            pieces = pieces + [lax.ppermute(x, "case", swap) for x in pieces]
            order = order + [m ^ bit for m in order]
            bit //= 2
        edges.append(boundary_columns(order, pick, pieces, flops))
    voltage, square, rate, worst = screen_branches(
        g, g_far, case_rows(tie_x[None], fault_z[None]), par, fd, edges, ahead, n_case
    )
    others = [
        lax.ppermute(worst, "case", [(i, i ^ m) for i in range(n_case)])
        for m in range(n_case - 1, 0, -1)
    ]
    relay_rate = relay_rates(square, rate, par)
    half_power, factor = curve_constants(curve)
    worst = functools.reduce(jnp.maximum, others, worst).reshape(-1)
    worst_rate = relay_of_square(worst, half_power, 1.0 / (factor * tds))
    return (voltage, relay_rate, worst_rate)


def solution(mesh):
    in_specs = (
        P("bus", None),
        P(),
        P("case"),
        P("case", None),
        P("case"),
        P("case"),
        P(),
        P("bus", None),
        P("bus"),
        P("bus"),
        P("bus"),
        P("bus"),
    )
    out_specs = (P("bus", "case"), P("bus", "case"), P("bus"))
    return jax.shard_map(
        per_device, mesh=mesh, in_specs=in_specs, out_specs=out_specs, check_vma=False
    )
```
